256 devices in a mesh: row: 32 (over z, x), col: 8 (over y, core).
Axes of the slice: x: 4, y: 4, z: 8, core: 2. Of those that a mesh axis runs over, the one named last changes fastest.
Arguments:
- blocks: bfloat16 [384, 16, 256, 256], P('row', 'col'), may hold values from -0.09375 to 0.09375
- neighbours: int32 [384, 16], P('row', 'col'), may hold values from 0 to 23, as said below
- start: bfloat16 [98304, 256], P(('row', 'col')), may hold values from -6 to 6
Outputs:
- basis: float32 [98304, 256], P(('row', 'col'))
- diagonal: float32 [256], replicated
The draws below stay inside these ranges and needn't reach their ends.
Inputs may be any that keep to these rules, and one draw needn't show every extreme that they name: The entries of one row of neighbours are distinct, so the slots of a block row name distinct block columns.
All inputs are finite; a program needn't handle non-finite values.
Results may differ from the reference program's by a relative error of at most 0.007.
Values may be sent and summed in bfloat16 or wider, within the bound.
No kernel may reach another device: no remote copies, remote signals or barrier semaphores. Data moves between devices by JAX's collectives and lax.ppermute only.
A program may use at most 64 MiB of HBM per device.

```python
import math
import jax
import jax.numpy as jnp
from jax import lax

BS = 256
K = 256
BR_DEV = 12
ITERS = 2
NEIGH = 16
HALF = 6
NBLK = 384
NROWS = 98304


def draw_neighbours(key, part):
    key = jax.random.fold_in(key, 7)
    width = 2 * BR_DEV
    scores = jax.random.randint(key, (NBLK, width), 0, 1 << 20) * width + jnp.arange(width, dtype=jnp.int32)[None, :]
    order = jnp.argsort(scores, axis=1).astype(jnp.int32)
    return order[:, :NEIGH]


def levels(own_key, extent, shards, least, high):
    def one(axis_at, parts):
        draws = jax.random.uniform(jax.random.fold_in(jax.random.fold_in(own_key, 6), axis_at), (parts,), jnp.float32, least / len(shards), high / len(shards))
        return jnp.repeat(jnp.exp(draws), extent[axis_at] // parts).reshape((-1,) + (1,) * (len(extent) - axis_at - 1))

    level = one(*shards[0])
    for cut in shards[1:]:
        level = level * one(*cut)
    return level


def bell_draw(key, extent, scale, bound, shards=(), held_as=jnp.bfloat16):
    values = jax.random.normal(key, extent, jnp.float32) * scale
    if len(shards) > 0:
        values = levels(key, extent, shards, -0.22, 0.18) * values
    return jnp.clip(values, min=-bound, max=bound).astype(held_as)


def setup_inputs(seed: int = 0) -> dict:
    key_list = jax.random.split(jax.random.key(seed), 4)
    return {
        "blocks": bell_draw(key_list[0], (NBLK, NEIGH, BS, BS), (NEIGH * BS) ** -0.5, 0.09375, ((0, 32), (1, 8))),
        "neighbours": draw_neighbours(jax.random.fold_in(key_list[3], 71), 0),
        "start": bell_draw(key_list[2], (NROWS, K), 1.0, 6.0, ((0, 256),)),
    }


def reference(blocks, neighbours, start):
    groups = NBLK // BR_DEV
    first = jnp.arange(NBLK, dtype=jnp.int32) // BR_DEV * BR_DEV - HALF
    columns = ((first[:, None] + neighbours) % NBLK).astype(jnp.int32)
    grouped = blocks.reshape(groups, BR_DEV, NEIGH, BS, BS)
    grouped_cols = columns.reshape(groups, BR_DEV, NEIGH)
    current = start
    for step in range(ITERS):
        stacked = current.reshape(NBLK, BS, K)

        def image(pair):
            tiles, cols = pair
            picked = stacked[cols]
            return jnp.einsum('rnab,rnbk->rak', tiles.astype(jnp.float32), picked.astype(jnp.float32))
        image_rows = lax.map(image, (grouped, grouped_cols)).reshape(groups, BR_DEV, BS, K).astype(jnp.bfloat16)

        def back(total, triple):
            tiles, cols, rows_y = triple
            terms = jnp.einsum('rnba,rbk->rnak', tiles.astype(jnp.float32), rows_y.astype(jnp.float32))
            return (total.at[cols.reshape(-1)].add(terms.reshape(-1, BS, K)), None)
        result, unused = lax.scan(back, jnp.zeros((NBLK, BS, K), jnp.float32), (grouped, grouped_cols, image_rows))
        result = result.reshape(NROWS, K)
        gram = jnp.dot(result.T.astype(jnp.float32), result.astype(jnp.float32), precision=lax.Precision.HIGHEST, preferred_element_type=jnp.float32)
        lower = jnp.linalg.cholesky(gram)
        basis = lax.linalg.triangular_solve(lower, result, left_side=False, lower=True, transpose_a=True)
        current = basis.astype(jnp.bfloat16)
    return (basis * math.sqrt(NROWS), jnp.diagonal(lower))
```

```python
import functools
import math

import jax
import jax.numpy as jnp
from jax import lax
from jax.experimental import pallas as pl
from jax.experimental.pallas import tpu as pltpu
from jax.sharding import PartitionSpec as P

ITERS = 2
PANEL = 64
GROUP = 4
HIGH = lax.Precision.HIGHEST


def band_kernel(cols, halves, slots, nb_ref, blk_ref, x_ref, out_ref, xwin, zacc, zbf, yref, sem):
    piece = x_ref.shape[0] // (2 * cols)
    side = 2 * blk_ref.shape[3]
    half = side // 2
    low = cols // 2 * piece
    places = []
    for c in range(cols):
        places.append((c * 2 * piece, low + c * piece))
        at = low + cols * piece + c * piece if c < cols // 2 else (c - cols // 2) * piece
        places.append((c * 2 * piece + piece, at))
    ins = [
        pltpu.make_async_copy(x_ref.at[pl.ds(a, piece)], xwin.at[pl.ds(b, piece)], sem.at[i])
        for i, (a, b) in enumerate(places)
    ]
    for copy in ins:
        copy.start()
    zacc[...] = jnp.zeros_like(zacc)
    for copy in ins:
        copy.wait()
    per = halves * slots
    for h in range(halves):

        def forward(s, acc):
            for n in range(slots):
                w = nb_ref[s * per + h * slots + n]
                x = xwin[pl.ds(pl.multiple_of(w * side, side), side), :]
                acc = acc + jnp.dot(blk_ref[s, h, n], x, preferred_element_type=jnp.float32)
            return acc

        acc = lax.fori_loop(0, cols, forward, jnp.zeros((half, xwin.shape[1]), jnp.float32))
        yref[h] = acc.astype(jnp.bfloat16)

    def back(s, carry):
        for h in range(halves):
            for n in range(slots):
                w = nb_ref[s * per + h * slots + n]
                term = lax.dot_general(
                    blk_ref[s, h, n],
                    yref[h],
                    (((0,), (0,)), ((), ())),
                    preferred_element_type=jnp.float32,
                )
                zacc[pl.ds(pl.multiple_of(w * side, side), side), :] += term
        return carry

    lax.fori_loop(0, cols, back, 0)
    outs = [
        pltpu.make_async_copy(zbf.at[pl.ds(b, piece)], out_ref.at[pl.ds(a, piece)], sem.at[i])
        for i, (a, b) in enumerate(places)
    ]
    for copy, (a, b) in zip(outs, places):
        zbf[pl.ds(b, piece), :] = zacc[pl.ds(b, piece), :].astype(jnp.bfloat16)
        copy.start()
    for copy in outs:
        copy.wait()


def band(nb, blk, x):
    cols, halves, slots, half, side = blk.shape
    width = x.shape[1]
    window = x.shape[0]
    return pl.pallas_call(
        functools.partial(band_kernel, cols, halves, slots),
        out_shape=jax.ShapeDtypeStruct(x.shape, jnp.bfloat16),
        in_specs=[
            pl.BlockSpec(memory_space=pltpu.SMEM),
            pl.BlockSpec(memory_space=pltpu.VMEM),
            pl.BlockSpec(memory_space=pl.ANY),
        ],
        out_specs=pl.BlockSpec(memory_space=pl.ANY),
        scratch_shapes=[
            pltpu.VMEM((window, width), jnp.bfloat16),
            pltpu.VMEM((window, width), jnp.float32),
            pltpu.VMEM((window, width), jnp.bfloat16),
            pltpu.VMEM((halves, half, width), jnp.bfloat16),
            pltpu.SemaphoreType.DMA((2 * cols,)),
        ],
        compiler_params=pltpu.CompilerParams(vmem_limit_bytes=40 * 2**20),
        name="band",
    )(nb, blk, x)


def gram_kernel(rs_ref, got_ref, z_ref, g_ref):
    piece = got_ref.shape[0]
    z = rs_ref[:piece, :].astype(jnp.float32) + got_ref[...].astype(jnp.float32)
    z_ref[...] = z
    g_ref[...] = lax.dot_general(
        z, z, (((0,), (0,)), ((), ())), precision=HIGH, preferred_element_type=jnp.float32
    )


def gram(rs, got):
    width = rs.shape[1]
    return pl.pallas_call(
        gram_kernel,
        out_shape=(
            jax.ShapeDtypeStruct(got.shape, jnp.float32),
            jax.ShapeDtypeStruct((width, width), jnp.float32),
        ),
        name="gram",
    )(rs, got)


def panel(tiles, start, count):
    lanes = 128
    at, offset = start // lanes, start % lanes
    rows = lax.broadcasted_iota(jnp.int32, (count, lanes), 0)
    pivots = jnp.ones((count, lanes), jnp.float32)
    for k in range(0, count, GROUP):
        columns = [
            jnp.broadcast_to(
                tiles[at][:, offset + k + j : offset + k + j + 1], (count, lanes)
            )
            for j in range(GROUP)
        ]
        heads = [[t[k + j : k + j + 1, :] for t in tiles] for j in range(GROUP)]
        terms = []
        for j in range(GROUP):
            pivot = columns[j][k + j : k + j + 1, :]
            inverse = 1.0 / pivot
            scaled = [h * inverse for h in heads[j]]
            below = jnp.where(rows > k + j, columns[j], 0.0)
            terms.append((below, scaled))
            pivots = jnp.where(rows == k + j, pivot, pivots)
            for i in range(j + 1, GROUP):
                factor = columns[j][k + i : k + i + 1, :]
                columns[i] = columns[i] - columns[j] * (factor * inverse)
                heads[i] = [h - factor * s for h, s in zip(heads[i], scaled)]
        for t in range(len(tiles)):
            total = tiles[t]
            for below, scaled in terms:
                total = total - below * scaled[t]
            tiles[t] = total
    scale = 1.0 / jnp.sqrt(pivots)
    return [t * scale for t in tiles]


def orthonormal_kernel(factor, g_ref, z_ref, q_ref, d_ref, m):
    width = g_ref.shape[0]
    lanes = 128
    m[:, :width] = g_ref[...]
    r = lax.broadcasted_iota(jnp.int32, (width, width), 0)
    c = lax.broadcasted_iota(jnp.int32, (width, width), 1)
    eye = (r == c).astype(jnp.float32)
    m[:, width:] = eye
    for start in range(0, width, PANEL):
        end = start + PANEL
        first = start // lanes
        used = list(range(first, width // lanes)) + list(
            range(width // lanes, width // lanes + (end + lanes - 1) // lanes)
        )
        tiles = [m[start:end, t * lanes : (t + 1) * lanes] for t in used]
        tiles = panel(tiles, start - first * lanes, PANEL)
        for t, value in zip(used, tiles):
            m[start:end, t * lanes : (t + 1) * lanes] = value
        if end < width:
            upper = jnp.concatenate(tiles, axis=1)
            left = upper[:, : width - first * lanes]
            update = lax.dot_general(
                left, upper, (((0,), (0,)), ((), ())), precision=HIGH,
                preferred_element_type=jnp.float32,
            )
            skip = end - first * lanes
            for i, t in enumerate(used):
                m[end:, t * lanes : (t + 1) * lanes] -= update[skip:, i * lanes : (i + 1) * lanes]
    d_ref[...] = jnp.sum(m[:, :width] * eye, axis=0, keepdims=True)
    q = lax.dot_general(
        z_ref[...], m[:, width:], (((1,), (1,)), ((), ())), precision=HIGH,
        preferred_element_type=jnp.float32,
    )
    q_ref[...] = (q * factor).astype(q_ref.dtype)


def orthonormal(g, z, dtype, factor):
    width = g.shape[0]
    return pl.pallas_call(
        functools.partial(orthonormal_kernel, factor),
        out_shape=(
            jax.ShapeDtypeStruct(z.shape, dtype),
            jax.ShapeDtypeStruct((1, width), jnp.float32),
        ),
        scratch_shapes=[pltpu.VMEM((width, 2 * width), jnp.float32)],
        name="orthonormal",
    )(g, z)


def exchange(value, mask, axis, count):
    return lax.ppermute(value, axis, [(i, i ^ mask) for i in range(count)])


def summed(value):
    cols = lax.axis_size("col")
    count = lax.axis_size("row")
    parts = lax.all_to_all(value, "col", 0, 0, tiled=True)
    part = jnp.sum(parts.reshape((cols, -1) + value.shape[1:]), axis=0)
    mask = 1
    while mask < count:
        part = part + exchange(part, mask, "row", count)
        mask *= 2
    return lax.all_to_all(jnp.tile(part, (cols, 1)), "col", 0, 0, tiled=True)


def per_device(blocks, neighbours, start):
    rows, slots, side, _ = blocks.shape
    cols = lax.axis_size("col")
    groups = lax.axis_size("row")
    piece, width = start.shape
    total_rows = piece * cols * groups
    half = side // 2
    halves = 2 * rows // cols

    def hop(g, c):
        return ((g - 1) % groups if c < cols // 2 else (g + 1) % groups) * cols + c

    out_hop = [(g * cols + c, hop(g, c)) for g in range(groups) for c in range(cols)]
    back_hop = [(b, a) for a, b in out_hop]

    sent = blocks.reshape(rows, slots, 2, half, side).transpose(0, 2, 1, 3, 4)
    sent = sent.reshape(cols, halves * slots * half, side)
    numbers = jnp.broadcast_to(neighbours[:, None, :], (rows, 2, slots))
    numbers = numbers.reshape(cols, 1, halves * slots).astype(jnp.bfloat16)
    numbers = jnp.pad(numbers, ((0, 0), (0, 15), (0, side - halves * slots)))
    sent = jnp.concatenate([sent, numbers], axis=1)
    got = lax.all_to_all(sent, "col", 0, 0, tiled=True)
    blk = got[:, :-16].reshape(cols, halves, slots, half, side)
    nb = got[:, -16, : halves * slots].astype(jnp.int32).reshape(-1)

    current = start
    for step in range(ITERS):
        halo = lax.ppermute(current, ("row", "col"), out_hop)
        window = lax.all_gather(
            jnp.concatenate([current, halo], axis=0), "col", axis=0, tiled=True
        )
        terms = band(nb, blk, window)
        mine = lax.psum_scatter(terms, "col", scatter_dimension=0, tiled=True)
        returned = lax.ppermute(mine[piece:], ("row", "col"), back_hop)
        z, local = gram(mine, returned)
        g = summed(local)
        last = step == ITERS - 1
        current, diagonal = orthonormal(
            g, z, jnp.float32 if last else jnp.bfloat16, math.sqrt(total_rows) if last else 1.0
        )
    return current, diagonal.reshape(width)


def solution(mesh):
    placed = (P("row", "col", None, None), P("row", "col"), P(("row", "col"), None))
    return jax.shard_map(
        per_device,
        mesh=mesh,
        in_specs=placed,
        out_specs=(P(("row", "col"), None), P()),
        check_vma=False,
    )
```

```python
import functools
import math

import jax
import jax.numpy as jnp
from jax import lax
from jax.experimental import pallas as pl
from jax.experimental.pallas import tpu as pltpu
from jax.sharding import PartitionSpec as P

ITERS = 2
PANEL = 64
GROUP = 8
HIGH = lax.Precision.HIGHEST
ANY = pl.BlockSpec(memory_space=pl.ANY)
SMEM = pl.BlockSpec(memory_space=pltpu.SMEM)
VMEM = pl.BlockSpec(memory_space=pltpu.VMEM)
BIG = 60 * 2**20


def sort_kernel(cols, halves, blk_ref, start_ref, *refs):
    outs, start_out = refs[:cols], refs[cols]
    held, rows, isem, osem = refs[cols + 1 :]
    first = pltpu.make_async_copy(start_ref, rows, isem.at[cols * halves])
    first.start()
    half = outs[0].shape[2]
    me = lax.axis_index("col")
    ins = []
    for m in range(cols):
        to = jnp.bitwise_xor(me, m)
        for h in range(halves):
            at = to * halves + h
            ins.append(
                pltpu.make_async_copy(
                    blk_ref.at[at // 2, :, pl.ds(pl.multiple_of(at % 2 * half, half), half), :],
                    held.at[m, h],
                    isem.at[m * halves + h],
                )
            )
    for copy in ins:
        copy.start()
    first.wait()
    copies = [pltpu.make_async_copy(rows, start_out, osem.at[cols])]
    copies[0].start()
    for m in range(cols):
        for copy in ins[m * halves : (m + 1) * halves]:
            copy.wait()
        copies.append(pltpu.make_async_copy(held.at[m], outs[m], osem.at[m]))
        copies[-1].start()
    for copy in copies:
        copy.wait()


def sort_blocks(blocks, start, cols):
    rows, slots, side, _ = blocks.shape
    halves = 2 * rows // cols
    shape = (halves, slots, side // 2, side)
    return pl.pallas_call(
        functools.partial(sort_kernel, cols, halves),
        out_shape=(jax.ShapeDtypeStruct(shape, blocks.dtype),) * cols
        + (jax.ShapeDtypeStruct(start.shape, start.dtype),),
        in_specs=[ANY, ANY],
        out_specs=(ANY,) * (cols + 1),
        scratch_shapes=[
            pltpu.VMEM((cols,) + shape, blocks.dtype),
            pltpu.VMEM(start.shape, start.dtype),
            pltpu.SemaphoreType.DMA((cols * halves + 1,)),
            pltpu.SemaphoreType.DMA((cols + 1,)),
        ],
        compiler_params=pltpu.CompilerParams(vmem_limit_bytes=BIG),
        name="sort_blocks",
    )(blocks, start)


def band_kernel(cols, nb_ref, *refs):
    blks, owns, halos = refs[:cols], refs[cols : 2 * cols], refs[2 * cols : 3 * cols]
    keep_h, send_h, keep_o, send_o = refs[3 * cols : 3 * cols + 4]
    blk, xwin, zacc, zbf, yref, isem, bsem, osem = refs[3 * cols + 4 :]
    piece, width = owns[0].shape
    halves, slots, half, side = blks[0].shape
    low = cols // 2 * piece
    me = lax.axis_index("col")
    odd = me % 2

    def own_at(c):
        return pl.multiple_of(low + c * piece, half)

    def halo_at(c):
        return pl.multiple_of(
            jnp.where(c < cols // 2, low + (cols + c) * piece, (c - cols // 2) * piece), half
        )

    xs, bs = [], []
    for m in range(cols):
        c = jnp.bitwise_xor(me, m)
        for i, (src, at) in enumerate(((owns[m], own_at(c)), (halos[m], halo_at(c)))):
            xs.append(pltpu.make_async_copy(src, xwin.at[pl.ds(at, piece)], isem.at[2 * m + i]))
        bs.append(pltpu.make_async_copy(blks[m], blk.at[m], bsem.at[m]))
    for copy in xs:
        copy.start()
    for copy in bs:
        copy.start()
    zacc[...] = jnp.zeros_like(zacc)
    for copy in xs:
        copy.wait()

    single = 2 - 2 * odd
    pair_row = (me * halves + odd) // 2
    single_row = (me * halves + single) // 2

    def places(m, n):
        base = m * (halves * cols // 2 * slots) + n
        a = nb_ref[base + pair_row * slots] * side
        b = nb_ref[base + single_row * slots] * side
        return pl.multiple_of(a, side), pl.multiple_of(b, side)

    acc = jnp.zeros((2 * half, width), jnp.float32)
    acc1 = jnp.zeros((half, width), jnp.float32)
    for m in range(cols):
        bs[m].wait()
        for n in range(slots):
            a, b = places(m, n)
            pair = blk[m, pl.ds(odd, 2), n].reshape(2 * half, side)
            acc += jnp.dot(pair, xwin[pl.ds(a, side), :], preferred_element_type=jnp.float32)
            acc1 += jnp.dot(
                blk[m, single, n], xwin[pl.ds(b, side), :], preferred_element_type=jnp.float32
            )
    yref[: 2 * half] = acc.astype(jnp.bfloat16)
    yref[2 * half :] = acc1.astype(jnp.bfloat16)
    y = yref[: 2 * half]
    y1 = yref[2 * half :]
    turned = (((0,), (0,)), ((), ()))

    def back(m, carry):
        for n in range(slots):
            a, b = places(m, n)
            pair = blk[m, pl.ds(odd, 2), n].reshape(2 * half, side)
            zacc[pl.ds(a, side), :] += lax.dot_general(
                pair, y, turned, preferred_element_type=jnp.float32
            )
            zacc[pl.ds(b, side), :] += lax.dot_general(
                blk[m, single, n], y1, turned, preferred_element_type=jnp.float32
            )
        return carry

    lax.fori_loop(0, cols, back, 0, unroll=4)
    outs = []
    for refs2, at_of in (((keep_h, send_h), halo_at), ((keep_o, send_o), own_at)):
        for j in (1, 0):
            for i in range(cols // 2):
                at = at_of(jnp.bitwise_xor(me, 2 * i + j))
                zbf[pl.ds(at, piece), :] = zacc[pl.ds(at, piece), :].astype(jnp.bfloat16)
                copy = pltpu.make_async_copy(
                    zbf.at[pl.ds(at, piece)], refs2[j].at[i], osem.at[len(outs)]
                )
                copy.start()
                outs.append(copy)
    for copy in outs:
        copy.wait()


def band(nb, blks, owns, halos):
    cols = len(blks)
    halves, slots, half, side = blks[0].shape
    piece, width = owns[0].shape
    window = 2 * cols * piece
    out = jax.ShapeDtypeStruct((cols // 2, piece, width), jnp.bfloat16)
    return pl.pallas_call(
        functools.partial(band_kernel, cols),
        out_shape=(out,) * 4,
        in_specs=[SMEM] + [ANY] * (3 * cols),
        out_specs=(ANY,) * 4,
        scratch_shapes=[
            pltpu.VMEM((cols, halves, slots, half, side), jnp.bfloat16),
            pltpu.VMEM((window, width), jnp.bfloat16),
            pltpu.VMEM((window, width), jnp.float32),
            pltpu.VMEM((window, width), jnp.bfloat16),
            pltpu.VMEM((halves * half, width), jnp.bfloat16),
            pltpu.SemaphoreType.DMA((2 * cols,)),
            pltpu.SemaphoreType.DMA((cols,)),
            pltpu.SemaphoreType.DMA((2 * cols,)),
        ],
        compiler_params=pltpu.CompilerParams(vmem_limit_bytes=BIG),
        cost_estimate=pl.CostEstimate(
            flops=4 * cols * halves * slots * half * side * width,
            bytes_accessed=12 * 2**20,
            transcendentals=0,
        ),
        name="band",
    )(nb, *blks, *owns, *halos)


def gram_kernel(*refs):
    parts, (z_ref, g_ref) = refs[:-2], refs[-2:]
    z = parts[0][...]
    for part in parts[1:]:
        z = z + part[...].astype(jnp.float32)
    z_ref[...] = z
    g_ref[...] = lax.dot_general(
        z, z, (((0,), (0,)), ((), ())), precision=HIGH, preferred_element_type=jnp.float32
    )


def gram(*parts):
    shape = parts[0].shape
    return pl.pallas_call(
        gram_kernel,
        out_shape=(
            jax.ShapeDtypeStruct(shape, jnp.float32),
            jax.ShapeDtypeStruct((shape[1], shape[1]), jnp.float32),
        ),
        name="gram",
    )(*parts)


def panel(tiles, start, count):
    lanes = 128
    at, offset = start // lanes, start % lanes
    rows = lax.broadcasted_iota(jnp.int32, (count, lanes), 0)
    pivots = jnp.ones((count, lanes), jnp.float32)
    for k in range(0, count, GROUP):
        columns = [
            jnp.broadcast_to(
                tiles[at][:, offset + k + j : offset + k + j + 1], (count, lanes)
            )
            for j in range(GROUP)
        ]
        heads = [[t[k + j : k + j + 1, :] for t in tiles] for j in range(GROUP)]
        terms = []
        for j in range(GROUP):
            pivot = columns[j][k + j : k + j + 1, :]
            inverse = 1.0 / pivot
            scaled = [h * inverse for h in heads[j]]
            below = jnp.where(rows > k + j, columns[j], 0.0)
            terms.append((below, scaled))
            pivots = jnp.where(rows == k + j, pivot, pivots)
            for i in range(j + 1, GROUP):
                factor = columns[j][k + i : k + i + 1, :]
                columns[i] = columns[i] - columns[j] * (factor * inverse)
                heads[i] = [h - factor * s for h, s in zip(heads[i], scaled)]
        for t in range(len(tiles)):
            total = tiles[t]
            for below, scaled in terms:
                total = total - below * scaled[t]
            tiles[t] = total
    scale = 1.0 / jnp.sqrt(pivots)
    return [t * scale for t in tiles]


def orthonormal_kernel(factor, g_ref, z_ref, q_ref, d_ref, m):
    width = g_ref.shape[0]
    lanes = 128
    m[:, :width] = g_ref[...]
    r = lax.broadcasted_iota(jnp.int32, (width, width), 0)
    c = lax.broadcasted_iota(jnp.int32, (width, width), 1)
    eye = (r == c).astype(jnp.float32)
    m[:, width:] = eye
    for start in range(0, width, PANEL):
        end = start + PANEL
        first = start // lanes
        used = list(range(first, width // lanes)) + list(
            range(width // lanes, width // lanes + (end + lanes - 1) // lanes)
        )
        tiles = [m[start:end, t * lanes : (t + 1) * lanes] for t in used]
        tiles = panel(tiles, start - first * lanes, PANEL)
        for t, value in zip(used, tiles):
            m[start:end, t * lanes : (t + 1) * lanes] = value
        if end < width:
            upper = jnp.concatenate(tiles, axis=1)
            left = upper[:, : width - first * lanes]
            update = lax.dot_general(
                left, upper, (((0,), (0,)), ((), ())), precision=HIGH,
                preferred_element_type=jnp.float32,
            )
            skip = end - first * lanes
            for i, t in enumerate(used):
                m[end:, t * lanes : (t + 1) * lanes] -= update[skip:, i * lanes : (i + 1) * lanes]
    d_ref[...] = jnp.sum(m[:, :width] * eye, axis=0, keepdims=True)
    q = lax.dot_general(
        z_ref[...], m[:, width:], (((1,), (1,)), ((), ())), precision=HIGH,
        preferred_element_type=jnp.float32,
    )
    q_ref[...] = (q * factor).astype(q_ref.dtype)


def orthonormal(g, z, dtype, factor):
    width = z.shape[1]
    return pl.pallas_call(
        functools.partial(orthonormal_kernel, factor),
        out_shape=(
            jax.ShapeDtypeStruct(z.shape, dtype),
            jax.ShapeDtypeStruct((1, width), jnp.float32),
        ),
        scratch_shapes=[pltpu.VMEM((width, 2 * width), jnp.float32)],
        name="orthonormal",
    )(g, z)


def exchange(value, mask, axis):
    return lax.ppermute(value, axis, [(i, i ^ mask) for i in range(lax.axis_size(axis))])


def masks_of(count):
    if count == 32:
        return (1, 3, 4, 8, 24)
    return tuple(1 << i for i in range(count.bit_length() - 1))


def summed(value):
    cols = lax.axis_size("col")
    parts = lax.all_to_all(value, "col", 0, 0, tiled=True)
    part = jnp.sum(parts.reshape((cols, -1) + value.shape[1:]), axis=0)
    for mask in masks_of(lax.axis_size("row")):
        part = part + exchange(part, mask, "row")
    return lax.all_to_all(jnp.tile(part, (cols, 1)), "col", 0, 0, tiled=True)


def collected(value, cols):
    held = value[None]
    mask = 1
    while mask < cols:
        held = jnp.concatenate([held, exchange(held, mask, "col")], axis=0)
        mask *= 2
    return held


def per_device(blocks, neighbours, start):
    cols = lax.axis_size("col")
    groups = lax.axis_size("row")
    piece, width = start.shape
    total_rows = piece * cols * groups
    chips = range(0, cols, 2)

    def hops(sign):
        pairs = []
        for g in range(groups):
            for c in range(cols):
                step = -sign if c < cols // 2 else sign
                pairs.append((g * cols + c, (g + step) % groups * cols + c))
        return pairs

    near, far = hops(1), hops(-1)

    def to_group(value, pairs):
        return lax.ppermute(value, ("row", "col"), pairs)

    *own_blocks, current = sort_blocks(blocks, start, cols)
    blks = None
    for step in range(ITERS):
        own_chips = {m: exchange(current, m, "col") if m else current for m in chips}
        if blks is None:
            blks = [own_blocks[0]] + [None] * (cols - 1)
            first = [m for m in range(2, cols) if m // 2 in (1, cols // 2 - 1)]
            for m in first:
                blks[m] = exchange(own_blocks[m], m, "col")
            own_chips, blks = lax.optimization_barrier((own_chips, blks))
        halo_chips = {m: to_group(own_chips[m], near if m < cols // 2 else far) for m in chips}
        if step == 0:
            for m in range(1, cols):
                if m not in first:
                    blks[m] = exchange(own_blocks[m], m, "col")
            nb = collected(neighbours.reshape(-1), cols).reshape(-1)
            own_chips, halo_chips, blks = lax.optimization_barrier((own_chips, halo_chips, blks))
        owns, halos = [], []
        for m in chips:
            owns += [own_chips[m], exchange(own_chips[m], 1, "col")]
        for m in chips:
            halos += [halo_chips[m], exchange(halo_chips[m], 1, "col")]
        keep_h, send_h, keep_o, send_o = band(nb, blks, owns, halos)

        def folded(keep, send):
            got = exchange(send, 1, "col")
            sums = [keep[i].astype(jnp.float32) + got[i].astype(jnp.float32) for i in range(cols // 2)]
            return [sums[0]] + [
                exchange(sums[m // 2].astype(jnp.bfloat16), m, "col") for m in chips if m
            ]

        halo_parts = folded(keep_h, send_h)
        halo_sum = halo_parts[0]
        for part in halo_parts[1:]:
            halo_sum = halo_sum + part.astype(jnp.float32)
        returned = to_group(halo_sum.astype(jnp.bfloat16), far)
        z, local = gram(*folded(keep_o, send_o), returned)
        g = summed(local)
        last = step == ITERS - 1
        current, diagonal = orthonormal(
            g, z, jnp.float32 if last else jnp.bfloat16, math.sqrt(total_rows) if last else 1.0
        )
    return current, diagonal.reshape(width)


def solution(mesh):
    placed = (P("row", "col", None, None), P("row", "col"), P(("row", "col"), None))
    return jax.shard_map(
        per_device,
        mesh=mesh,
        in_specs=placed,
        out_specs=(P(("row", "col"), None), P()),
        check_vma=False,
    )
```

```python
import functools
import math

import jax
import jax.numpy as jnp
from jax import lax
from jax.experimental import pallas as pl
from jax.experimental.pallas import tpu as pltpu
from jax.sharding import PartitionSpec as P

ITERS = 2
PANEL = 64
GROUP = 8
HIGH = lax.Precision.HIGHEST
ANY = pl.BlockSpec(memory_space=pl.ANY)
SMEM = pl.BlockSpec(memory_space=pltpu.SMEM)
VMEM = pl.BlockSpec(memory_space=pltpu.VMEM)
BIG = 60 * 2**20


def sort_kernel(cols, halves, blk_ref, start_ref, *refs):
    outs, start_out = refs[:cols], refs[cols]
    held, rows, isem, osem = refs[cols + 1 :]
    first = pltpu.make_async_copy(start_ref, rows, isem.at[cols * halves])
    first.start()
    half = outs[0].shape[2]
    me = lax.axis_index("col")
    ins = []
    for m in range(cols):
        to = jnp.bitwise_xor(me, m)
        for h in range(halves):
            at = to * halves + h
            ins.append(
                pltpu.make_async_copy(
                    blk_ref.at[at // 2, :, pl.ds(pl.multiple_of(at % 2 * half, half), half), :],
                    held.at[m, h],
                    isem.at[m * halves + h],
                )
            )
    for copy in ins:
        copy.start()
    first.wait()
    copies = [pltpu.make_async_copy(rows, start_out, osem.at[cols])]
    copies[0].start()
    for m in range(cols):
        for copy in ins[m * halves : (m + 1) * halves]:
            copy.wait()
        copies.append(pltpu.make_async_copy(held.at[m], outs[m], osem.at[m]))
        copies[-1].start()
    for copy in copies:
        copy.wait()


def sort_blocks(blocks, start, cols):
    rows, slots, side, _ = blocks.shape
    halves = 2 * rows // cols
    shape = (halves, slots, side // 2, side)
    return pl.pallas_call(
        functools.partial(sort_kernel, cols, halves),
        out_shape=(jax.ShapeDtypeStruct(shape, blocks.dtype),) * cols
        + (jax.ShapeDtypeStruct(start.shape, start.dtype),),
        in_specs=[ANY, ANY],
        out_specs=(ANY,) * (cols + 1),
        scratch_shapes=[
            pltpu.VMEM((cols,) + shape, blocks.dtype),
            pltpu.VMEM(start.shape, start.dtype),
            pltpu.SemaphoreType.DMA((cols * halves + 1,)),
            pltpu.SemaphoreType.DMA((cols + 1,)),
        ],
        compiler_params=pltpu.CompilerParams(vmem_limit_bytes=BIG),
        name="sort_blocks",
    )(blocks, start)


def band_kernel(cols, nb_ref, *refs):
    blks, owns, halos = refs[:cols], refs[cols : 2 * cols], refs[2 * cols : 3 * cols]
    keep_h, send_h, keep_o, send_o = refs[3 * cols : 3 * cols + 4]
    blk, xwin, zacc, zbf, yref, isem, bsem, osem = refs[3 * cols + 4 :]
    piece, width = owns[0].shape
    halves, slots, half, side = blks[0].shape
    low = cols // 2 * piece
    me = lax.axis_index("col")
    odd = me % 2

    def own_at(c):
        return pl.multiple_of(low + c * piece, half)

    def halo_at(c):
        return pl.multiple_of(
            jnp.where(c < cols // 2, low + (cols + c) * piece, (c - cols // 2) * piece), half
        )

    xs, bs = [], []
    for m in range(cols):
        c = jnp.bitwise_xor(me, m)
        for i, (src, at) in enumerate(((owns[m], own_at(c)), (halos[m], halo_at(c)))):
            xs.append(pltpu.make_async_copy(src, xwin.at[pl.ds(at, piece)], isem.at[2 * m + i]))
        bs.append(pltpu.make_async_copy(blks[m], blk.at[m], bsem.at[m]))
    for copy in xs:
        copy.start()
    for copy in bs:
        copy.start()
    zacc[...] = jnp.zeros_like(zacc)
    for copy in xs:
        copy.wait()

    single = 2 - 2 * odd
    pair_row = (me * halves + odd) // 2
    single_row = (me * halves + single) // 2

    def places(m, n):
        base = m * (halves * cols // 2 * slots) + n
        a = nb_ref[base + pair_row * slots] * side
        b = nb_ref[base + single_row * slots] * side
        return pl.multiple_of(a, side), pl.multiple_of(b, side)

    acc = jnp.zeros((2 * half, width), jnp.float32)
    acc1 = jnp.zeros((half, width), jnp.float32)
    for m in range(cols):
        bs[m].wait()
        for n in range(slots):
            a, b = places(m, n)
            pair = blk[m, pl.ds(odd, 2), n].reshape(2 * half, side)
            acc += jnp.dot(pair, xwin[pl.ds(a, side), :], preferred_element_type=jnp.float32)
            acc1 += jnp.dot(
                blk[m, single, n], xwin[pl.ds(b, side), :], preferred_element_type=jnp.float32
            )
    yref[: 2 * half] = acc.astype(jnp.bfloat16)
    yref[2 * half :] = acc1.astype(jnp.bfloat16)
    y = yref[: 2 * half]
    y1 = yref[2 * half :]
    turned = (((0,), (0,)), ((), ()))

    def back(m, carry):
        for n in range(slots):
            a, b = places(m, n)
            pair = blk[m, pl.ds(odd, 2), n].reshape(2 * half, side)
            zacc[pl.ds(a, side), :] += lax.dot_general(
                pair, y, turned, preferred_element_type=jnp.float32
            )
            zacc[pl.ds(b, side), :] += lax.dot_general(
                blk[m, single, n], y1, turned, preferred_element_type=jnp.float32
            )
        return carry

    lax.fori_loop(0, cols, back, 0, unroll=4)
    outs = []
    for refs2, at_of in (((keep_h, send_h), halo_at), ((keep_o, send_o), own_at)):
        for j in (1, 0):
            for i in range(cols // 2):
                at = at_of(jnp.bitwise_xor(me, 2 * i + j))
                zbf[pl.ds(at, piece), :] = zacc[pl.ds(at, piece), :].astype(jnp.bfloat16)
                copy = pltpu.make_async_copy(
                    zbf.at[pl.ds(at, piece)], refs2[j].at[i], osem.at[len(outs)]
                )
                copy.start()
                outs.append(copy)
    for copy in outs:
        copy.wait()


def band(nb, blks, owns, halos):
    cols = len(blks)
    halves, slots, half, side = blks[0].shape
    piece, width = owns[0].shape
    window = 2 * cols * piece
    out = jax.ShapeDtypeStruct((cols // 2, piece, width), jnp.bfloat16)
    return pl.pallas_call(
        functools.partial(band_kernel, cols),
        out_shape=(out,) * 4,
        in_specs=[SMEM] + [ANY] * (3 * cols),
        out_specs=(ANY,) * 4,
        scratch_shapes=[
            pltpu.VMEM((cols, halves, slots, half, side), jnp.bfloat16),
            pltpu.VMEM((window, width), jnp.bfloat16),
            pltpu.VMEM((window, width), jnp.float32),
            pltpu.VMEM((window, width), jnp.bfloat16),
            pltpu.VMEM((halves * half, width), jnp.bfloat16),
            pltpu.SemaphoreType.DMA((2 * cols,)),
            pltpu.SemaphoreType.DMA((cols,)),
            pltpu.SemaphoreType.DMA((2 * cols,)),
        ],
        compiler_params=pltpu.CompilerParams(vmem_limit_bytes=BIG),
        cost_estimate=pl.CostEstimate(
            flops=4 * cols * halves * slots * half * side * width,
            bytes_accessed=12 * 2**20,
            transcendentals=0,
        ),
        name="band",
    )(nb, *blks, *owns, *halos)


def gram_kernel(*refs):
    parts, (z_ref, g_ref) = refs[:-2], refs[-2:]
    z = parts[0][...]
    for part in parts[1:]:
        z = z + part[...].astype(jnp.float32)
    z_ref[...] = z
    g_ref[...] = lax.dot_general(
        z, z, (((0,), (0,)), ((), ())), precision=HIGH, preferred_element_type=jnp.float32
    )


def gram(*parts):
    shape = parts[0].shape
    return pl.pallas_call(
        gram_kernel,
        out_shape=(
            jax.ShapeDtypeStruct(shape, jnp.float32),
            jax.ShapeDtypeStruct((shape[1], shape[1]), jnp.float32),
        ),
        name="gram",
    )(*parts)


def panel(tiles, start, count):
    lanes = 128
    at, offset = start // lanes, start % lanes
    rows = lax.broadcasted_iota(jnp.int32, (count, lanes), 0)
    pivots = jnp.ones((count, lanes), jnp.float32)
    for k in range(0, count, GROUP):
        columns = [
            jnp.broadcast_to(
                tiles[at][:, offset + k + j : offset + k + j + 1], (count, lanes)
            )
            for j in range(GROUP)
        ]
        heads = [[t[k + j : k + j + 1, :] for t in tiles] for j in range(GROUP)]
        terms = []
        for j in range(GROUP):
            pivot = columns[j][k + j : k + j + 1, :]
            inverse = 1.0 / pivot
            scaled = [h * inverse for h in heads[j]]
            below = jnp.where(rows > k + j, columns[j], 0.0)
            terms.append((below, scaled))
            pivots = jnp.where(rows == k + j, pivot, pivots)
            for i in range(j + 1, GROUP):
                factor = columns[j][k + i : k + i + 1, :]
                columns[i] = columns[i] - columns[j] * (factor * inverse)
                heads[i] = [h - factor * s for h, s in zip(heads[i], scaled)]
        for t in range(len(tiles)):
            total = tiles[t]
            for below, scaled in terms:
                total = total - below * scaled[t]
            tiles[t] = total
    scale = 1.0 / jnp.sqrt(pivots)
    return [t * scale for t in tiles]


def orthonormal_kernel(factor, g_ref, z_ref, q_ref, d_ref, m):
    width = g_ref.shape[0]
    lanes = 128
    m[:, :width] = g_ref[...]
    r = lax.broadcasted_iota(jnp.int32, (width, width), 0)
    c = lax.broadcasted_iota(jnp.int32, (width, width), 1)
    eye = (r == c).astype(jnp.float32)
    m[:, width:] = eye
    for start in range(0, width, PANEL):
        end = start + PANEL
        first = start // lanes
        used = list(range(first, width // lanes)) + list(
            range(width // lanes, width // lanes + (end + lanes - 1) // lanes)
        )
        tiles = [m[start:end, t * lanes : (t + 1) * lanes] for t in used]
        tiles = panel(tiles, start - first * lanes, PANEL)
        for t, value in zip(used, tiles):
            m[start:end, t * lanes : (t + 1) * lanes] = value
        if end < width:
            upper = jnp.concatenate(tiles, axis=1)
            left = upper[:, : width - first * lanes]
            update = lax.dot_general(
                left, upper, (((0,), (0,)), ((), ())), precision=HIGH,
                preferred_element_type=jnp.float32,
            )
            skip = end - first * lanes
            for i, t in enumerate(used):
                m[end:, t * lanes : (t + 1) * lanes] -= update[skip:, i * lanes : (i + 1) * lanes]
    d_ref[...] = jnp.sum(m[:, :width] * eye, axis=0, keepdims=True)
    q = lax.dot_general(
        z_ref[...], m[:, width:], (((1,), (1,)), ((), ())), precision=HIGH,
        preferred_element_type=jnp.float32,
    )
    q_ref[...] = (q * factor).astype(q_ref.dtype)


def orthonormal(g, z, dtype, factor):
    width = z.shape[1]
    return pl.pallas_call(
        functools.partial(orthonormal_kernel, factor),
        out_shape=(
            jax.ShapeDtypeStruct(z.shape, dtype),
            jax.ShapeDtypeStruct((1, width), jnp.float32),
        ),
        scratch_shapes=[pltpu.VMEM((width, 2 * width), jnp.float32)],
        name="orthonormal",
    )(g, z)


def exchange(value, mask, axis):
    return lax.ppermute(value, axis, [(i, i ^ mask) for i in range(lax.axis_size(axis))])


def masks_of(count):
    if count == 32:
        return (1, 3, 4, 8, 24)
    return tuple(1 << i for i in range(count.bit_length() - 1))


def summed(value):
    cols = lax.axis_size("col")
    parts = lax.all_to_all(value, "col", 0, 0, tiled=True)
    part = jnp.sum(parts.reshape((cols, -1) + value.shape[1:]), axis=0)
    for mask in masks_of(lax.axis_size("row")):
        part = part + exchange(part, mask, "row")
    return lax.all_to_all(jnp.tile(part, (cols, 1)), "col", 0, 0, tiled=True)


def collected(value, cols):
    held = value[None]
    mask = 1
    while mask < cols:
        held = jnp.concatenate([held, exchange(held, mask, "col")], axis=0)
        mask *= 2
    return held


def per_device(blocks, neighbours, start):
    cols = lax.axis_size("col")
    groups = lax.axis_size("row")
    piece, width = start.shape
    total_rows = piece * cols * groups
    chips = range(0, cols, 2)

    def hops(sign):
        pairs = []
        for g in range(groups):
            for c in range(cols):
                step = -sign if c < cols // 2 else sign
                pairs.append((g * cols + c, (g + step) % groups * cols + c))
        return pairs

    near, far = hops(1), hops(-1)

    def to_group(value, pairs):
        return lax.ppermute(value, ("row", "col"), pairs)

    *own_blocks, current = sort_blocks(blocks, start, cols)
    blks = None
    for step in range(ITERS):
        own_chips = {m: exchange(current, m, "col") if m else current for m in chips}
        if blks is None:
            blks = list(own_blocks)
            first = [1, 2, cols - 2]
            for m in first:
                blks[m] = exchange(own_blocks[m], m, "col")
            nb = collected(neighbours.reshape(-1), cols).reshape(-1)
            own_chips, blks, nb = lax.optimization_barrier((own_chips, blks, nb))
        halo_chips = {m: to_group(own_chips[m], near if m < cols // 2 else far) for m in chips}
        if step == 0:
            for m in range(1, cols):
                if m not in first:
                    blks[m] = exchange(blks[m], m, "col")
            halo_chips, blks = lax.optimization_barrier((halo_chips, blks))
        owns, halos = [], []
        for m in chips:
            owns += [own_chips[m], exchange(own_chips[m], 1, "col")]
        for m in chips:
            halos += [halo_chips[m], exchange(halo_chips[m], 1, "col")]
        keep_h, send_h, keep_o, send_o = band(nb, blks, owns, halos)

        def folded(keep, send):
            got = exchange(send, 1, "col")
            sums = [keep[i].astype(jnp.float32) + got[i].astype(jnp.float32) for i in range(cols // 2)]
            return [sums[0]] + [
                exchange(sums[m // 2].astype(jnp.bfloat16), m, "col") for m in chips if m
            ]

        halo_parts = folded(keep_h, send_h)
        halo_sum = halo_parts[0]
        for part in halo_parts[1:]:
            halo_sum = halo_sum + part.astype(jnp.float32)
        returned = to_group(halo_sum.astype(jnp.bfloat16), far)
        z, local = gram(*folded(keep_o, send_o), returned)
        g = summed(local)
        last = step == ITERS - 1
        current, diagonal = orthonormal(
            g, z, jnp.float32 if last else jnp.bfloat16, math.sqrt(total_rows) if last else 1.0
        )
    return current, diagonal.reshape(width)


def solution(mesh):
    placed = (P("row", "col", None, None), P("row", "col"), P(("row", "col"), None))
    return jax.shard_map(
        per_device,
        mesh=mesh,
        in_specs=placed,
        out_specs=(P(("row", "col"), None), P()),
        check_vma=False,
    )
```

```python
import functools
import math

import jax
import jax.numpy as jnp
from jax import lax
from jax.experimental import pallas as pl
from jax.experimental.pallas import tpu as pltpu
from jax.sharding import PartitionSpec as P

ITERS = 2
PANEL = 64
GROUP = 8
HIGH = lax.Precision.HIGHEST
ANY = pl.BlockSpec(memory_space=pl.ANY)
SMEM = pl.BlockSpec(memory_space=pltpu.SMEM)
VMEM = pl.BlockSpec(memory_space=pltpu.VMEM)
BIG = 60 * 2**20


def sort_kernel(cols, halves, slots, nb_ref, blk_ref, start_ref, *refs):
    outs, start_out = refs[: cols // 2], refs[cols // 2]
    held, rows, isem, osem = refs[cols // 2 + 1 :]
    half = held.shape[4]
    piece, width = start_ref.shape
    me = lax.axis_index("col")
    first = pltpu.make_async_copy(start_ref, rows.at[pl.ds(0, piece)], isem.at[cols * halves])
    first.start()
    ins = []
    for m in range(cols):
        to = jnp.bitwise_xor(me, m)
        for h in range(halves):
            at = to * halves + h
            ins.append(
                pltpu.make_async_copy(
                    blk_ref.at[at // 2, :, pl.ds(pl.multiple_of(at % 2 * half, half), half), :],
                    held.at[m // 2, m % 2, h],
                    isem.at[m * halves + h],
                )
            )
    for copy in ins:
        copy.start()
    lane = lax.broadcasted_iota(jnp.int32, (16, width), 1)
    numbers = jnp.zeros((16, width), jnp.float32)
    for i in range(halves * cols // 2):
        for n in range(slots):
            value = nb_ref[i, n].astype(jnp.float32)
            numbers = jnp.where(lane == i * slots + n, value, numbers)
    rows[piece:, :] = numbers.astype(rows.dtype)
    first.wait()
    copies = [pltpu.make_async_copy(rows, start_out, osem.at[cols // 2])]
    copies[0].start()
    for i in range(cols // 2):
        for copy in ins[2 * i * halves : 2 * (i + 1) * halves]:
            copy.wait()
        copies.append(pltpu.make_async_copy(held.at[i], outs[i], osem.at[i]))
        copies[-1].start()
    for copy in copies:
        copy.wait()


def sort_blocks(neighbours, blocks, start, cols):
    rows, slots, side, _ = blocks.shape
    halves = 2 * rows // cols
    piece, width = start.shape
    shape = (2, halves, slots, side // 2, side)
    return pl.pallas_call(
        functools.partial(sort_kernel, cols, halves, slots),
        out_shape=(jax.ShapeDtypeStruct(shape, blocks.dtype),) * (cols // 2)
        + (jax.ShapeDtypeStruct((piece + 16, width), start.dtype),),
        in_specs=[SMEM, ANY, ANY],
        out_specs=(ANY,) * (cols // 2 + 1),
        scratch_shapes=[
            pltpu.VMEM((cols // 2,) + shape, blocks.dtype),
            pltpu.VMEM((piece + 16, width), start.dtype),
            pltpu.SemaphoreType.DMA((cols * halves + 1,)),
            pltpu.SemaphoreType.DMA((cols // 2 + 1,)),
        ],
        compiler_params=pltpu.CompilerParams(vmem_limit_bytes=BIG),
        name="sort_blocks",
    )(neighbours, blocks, start)


def band_kernel(cols, nb_ref, *refs):
    blks, owns, halos = refs[:cols], refs[cols : 2 * cols], refs[2 * cols : 3 * cols]
    keep_h, send_h, keep_o, send_o = refs[3 * cols : 3 * cols + 4]
    blk, xwin, zacc, zbf, yref, isem, bsem, osem = refs[3 * cols + 4 :]
    piece, width = keep_h.shape[1:]
    _, halves, slots, half, side = blks[0].shape
    low = cols // 2 * piece
    me = lax.axis_index("col")
    odd = me % 2

    def own_at(c):
        return pl.multiple_of(low + c * piece, half)

    def halo_at(c):
        return pl.multiple_of(
            jnp.where(c < cols // 2, low + (cols + c) * piece, (c - cols // 2) * piece), half
        )

    xs, bs = [], []
    for m in range(cols):
        c = jnp.bitwise_xor(me, m)
        for i, (src, at) in enumerate(((owns[m], own_at(c)), (halos[m], halo_at(c)))):
            xs.append(pltpu.make_async_copy(src.at[pl.ds(0, piece)], xwin.at[pl.ds(at, piece)], isem.at[2 * m + i]))
        bs.append(pltpu.make_async_copy(blks[m].at[m % 2], blk.at[m], bsem.at[m]))
    for copy in xs:
        copy.start()
    for copy in bs:
        copy.start()
    zacc[...] = jnp.zeros_like(zacc)
    for copy in xs:
        copy.wait()

    single = 2 - 2 * odd
    pair_row = (me * halves + odd) // 2
    single_row = (me * halves + single) // 2

    def places(m, n):
        base = m * (halves * cols // 2 * slots) + n
        a = nb_ref[base + pair_row * slots] * side
        b = nb_ref[base + single_row * slots] * side
        return pl.multiple_of(a, side), pl.multiple_of(b, side)

    acc = jnp.zeros((2 * half, width), jnp.float32)
    acc1 = jnp.zeros((half, width), jnp.float32)
    for m in range(cols):
        bs[m].wait()
        for n in range(slots):
            a, b = places(m, n)
            pair = blk[m, pl.ds(odd, 2), n].reshape(2 * half, side)
            acc += jnp.dot(pair, xwin[pl.ds(a, side), :], preferred_element_type=jnp.float32)
            acc1 += jnp.dot(
                blk[m, single, n], xwin[pl.ds(b, side), :], preferred_element_type=jnp.float32
            )
    yref[: 2 * half] = acc.astype(jnp.bfloat16)
    yref[2 * half :] = acc1.astype(jnp.bfloat16)
    y = yref[: 2 * half]
    y1 = yref[2 * half :]
    turned = (((0,), (0,)), ((), ()))

    def back(m, carry):
        for n in range(slots):
            a, b = places(m, n)
            pair = blk[m, pl.ds(odd, 2), n].reshape(2 * half, side)
            zacc[pl.ds(a, side), :] += lax.dot_general(
                pair, y, turned, preferred_element_type=jnp.float32
            )
            zacc[pl.ds(b, side), :] += lax.dot_general(
                blk[m, single, n], y1, turned, preferred_element_type=jnp.float32
            )
        return carry

    lax.fori_loop(0, cols, back, 0, unroll=4)
    outs = []
    for refs2, at_of in (((keep_h, send_h), halo_at), ((keep_o, send_o), own_at)):
        for j in (1, 0):
            for i in range(cols // 2):
                at = at_of(jnp.bitwise_xor(me, 2 * i + j))
                zbf[pl.ds(at, piece), :] = zacc[pl.ds(at, piece), :].astype(jnp.bfloat16)
                copy = pltpu.make_async_copy(
                    zbf.at[pl.ds(at, piece)], refs2[j].at[i], osem.at[len(outs)]
                )
                copy.start()
                outs.append(copy)
    for copy in outs:
        copy.wait()


def band(nb, blks, owns, halos):
    cols = len(blks)
    _, halves, slots, half, side = blks[0].shape
    width = owns[0].shape[1]
    piece = halves * half
    window = 2 * cols * piece
    out = jax.ShapeDtypeStruct((cols // 2, piece, width), jnp.bfloat16)
    return pl.pallas_call(
        functools.partial(band_kernel, cols),
        out_shape=(out,) * 4,
        in_specs=[SMEM] + [ANY] * (3 * cols),
        out_specs=(ANY,) * 4,
        scratch_shapes=[
            pltpu.VMEM((cols, halves, slots, half, side), jnp.bfloat16),
            pltpu.VMEM((window, width), jnp.bfloat16),
            pltpu.VMEM((window, width), jnp.float32),
            pltpu.VMEM((window, width), jnp.bfloat16),
            pltpu.VMEM((halves * half, width), jnp.bfloat16),
            pltpu.SemaphoreType.DMA((2 * cols,)),
            pltpu.SemaphoreType.DMA((cols,)),
            pltpu.SemaphoreType.DMA((2 * cols,)),
        ],
        compiler_params=pltpu.CompilerParams(vmem_limit_bytes=BIG),
        cost_estimate=pl.CostEstimate(
            flops=4 * cols * halves * slots * half * side * width,
            bytes_accessed=12 * 2**20,
            transcendentals=0,
        ),
        name="band",
    )(nb, *blks, *owns, *halos)


def gram_kernel(*refs):
    parts, (z_ref, g_ref) = refs[:-2], refs[-2:]
    z = parts[0][...]
    for part in parts[1:]:
        z = z + part[...].astype(jnp.float32)
    z_ref[...] = z
    g_ref[...] = lax.dot_general(
        z, z, (((0,), (0,)), ((), ())), precision=HIGH, preferred_element_type=jnp.float32
    )


def gram(*parts):
    shape = parts[0].shape
    return pl.pallas_call(
        gram_kernel,
        out_shape=(
            jax.ShapeDtypeStruct(shape, jnp.float32),
            jax.ShapeDtypeStruct((shape[1], shape[1]), jnp.float32),
        ),
        name="gram",
    )(*parts)


def panel(tiles, start, count):
    lanes = 128
    at, offset = start // lanes, start % lanes
    rows = lax.broadcasted_iota(jnp.int32, (count, lanes), 0)
    pivots = jnp.ones((count, lanes), jnp.float32)
    for k in range(0, count, GROUP):
        columns = [
            jnp.broadcast_to(
                tiles[at][:, offset + k + j : offset + k + j + 1], (count, lanes)
            )
            for j in range(GROUP)
        ]
        heads = [[t[k + j : k + j + 1, :] for t in tiles] for j in range(GROUP)]
        terms = []
        for j in range(GROUP):
            pivot = columns[j][k + j : k + j + 1, :]
            inverse = 1.0 / pivot
            scaled = [h * inverse for h in heads[j]]
            below = jnp.where(rows > k + j, columns[j], 0.0)
            terms.append((below, scaled))
            pivots = jnp.where(rows == k + j, pivot, pivots)
            for i in range(j + 1, GROUP):
                factor = columns[j][k + i : k + i + 1, :]
                columns[i] = columns[i] - columns[j] * (factor * inverse)
                heads[i] = [h - factor * s for h, s in zip(heads[i], scaled)]
        for t in range(len(tiles)):
            total = tiles[t]
            for below, scaled in terms:
                total = total - below * scaled[t]
            tiles[t] = total
    scale = 1.0 / jnp.sqrt(pivots)
    return [t * scale for t in tiles]


def orthonormal_kernel(factor, g_ref, z_ref, q_ref, d_ref, m):
    width = g_ref.shape[0]
    lanes = 128
    m[:, :width] = g_ref[...]
    r = lax.broadcasted_iota(jnp.int32, (width, width), 0)
    c = lax.broadcasted_iota(jnp.int32, (width, width), 1)
    eye = (r == c).astype(jnp.float32)
    m[:, width:] = eye
    for start in range(0, width, PANEL):
        end = start + PANEL
        first = start // lanes
        used = list(range(first, width // lanes)) + list(
            range(width // lanes, width // lanes + (end + lanes - 1) // lanes)
        )
        tiles = [m[start:end, t * lanes : (t + 1) * lanes] for t in used]
        tiles = panel(tiles, start - first * lanes, PANEL)
        for t, value in zip(used, tiles):
            m[start:end, t * lanes : (t + 1) * lanes] = value
        if end < width:
            upper = jnp.concatenate(tiles, axis=1)
            left = upper[:, : width - first * lanes]
            update = lax.dot_general(
                left, upper, (((0,), (0,)), ((), ())), precision=HIGH,
                preferred_element_type=jnp.float32,
            )
            skip = end - first * lanes
            for i, t in enumerate(used):
                m[end:, t * lanes : (t + 1) * lanes] -= update[skip:, i * lanes : (i + 1) * lanes]
    d_ref[...] = jnp.sum(m[:, :width] * eye, axis=0, keepdims=True)
    q = lax.dot_general(
        z_ref[...], m[:, width:], (((1,), (1,)), ((), ())), precision=HIGH,
        preferred_element_type=jnp.float32,
    )
    q_ref[...] = (q * factor).astype(q_ref.dtype)


def orthonormal(g, z, dtype, factor):
    width = z.shape[1]
    return pl.pallas_call(
        functools.partial(orthonormal_kernel, factor),
        out_shape=(
            jax.ShapeDtypeStruct(z.shape, dtype),
            jax.ShapeDtypeStruct((1, width), jnp.float32),
        ),
        scratch_shapes=[pltpu.VMEM((width, 2 * width), jnp.float32)],
        name="orthonormal",
    )(g, z)


def exchange(value, mask, axis):
    return lax.ppermute(value, axis, [(i, i ^ mask) for i in range(lax.axis_size(axis))])


def masks_of(count):
    if count == 32:
        return (1, 3, 4, 8, 24)
    return tuple(1 << i for i in range(count.bit_length() - 1))


def summed(value):
    cols = lax.axis_size("col")
    parts = lax.all_to_all(value, "col", 0, 0, tiled=True)
    part = jnp.sum(parts.reshape((cols, -1) + value.shape[1:]), axis=0)
    for mask in masks_of(lax.axis_size("row")):
        part = part + exchange(part, mask, "row")
    return lax.all_to_all(jnp.tile(part, (cols, 1)), "col", 0, 0, tiled=True)


def per_device(blocks, neighbours, start):
    cols = lax.axis_size("col")
    groups = lax.axis_size("row")
    piece, width = start.shape
    total_rows = piece * cols * groups
    chips = range(0, cols, 2)

    def hops(sign):
        pairs = []
        for g in range(groups):
            for c in range(cols):
                step = -sign if c < cols // 2 else sign
                pairs.append((g * cols + c, (g + step) % groups * cols + c))
        return pairs

    near, far = hops(1), hops(-1)

    def to_group(value, pairs):
        return lax.ppermute(value, ("row", "col"), pairs)

    *sorted_blocks, current = sort_blocks(neighbours, blocks, start, cols)
    blks = []
    for m in chips:
        got = exchange(sorted_blocks[m // 2], m, "col") if m else sorted_blocks[0]
        blks += [got, exchange(got, 1, "col")]
    for step in range(ITERS):
        own_chips = {m: exchange(current, m, "col") if m else current for m in chips}
        halo_chips = {m: to_group(own_chips[m], near if m < cols // 2 else far) for m in chips}
        owns, halos = [], []
        for m in chips:
            owns += [own_chips[m], exchange(own_chips[m], 1, "col")]
        for m in chips:
            halos += [halo_chips[m], exchange(halo_chips[m], 1, "col")]
        if step == 0:
            nb = jnp.concatenate([part[piece, : neighbours.size] for part in owns]).astype(jnp.int32)
        keep_h, send_h, keep_o, send_o = band(nb, blks, owns, halos)

        def folded(keep, send):
            got = exchange(send, 1, "col")
            sums = [keep[i].astype(jnp.float32) + got[i].astype(jnp.float32) for i in range(cols // 2)]
            return [sums[0]] + [
                exchange(sums[m // 2].astype(jnp.bfloat16), m, "col") for m in chips if m
            ]

        halo_parts = folded(keep_h, send_h)
        halo_sum = halo_parts[0]
        for part in halo_parts[1:]:
            halo_sum = halo_sum + part.astype(jnp.float32)
        returned = to_group(halo_sum.astype(jnp.bfloat16), far)
        z, local = gram(*folded(keep_o, send_o), returned)
        g = summed(local)
        last = step == ITERS - 1
        current, diagonal = orthonormal(
            g, z, jnp.float32 if last else jnp.bfloat16, math.sqrt(total_rows) if last else 1.0
        )
    return current, diagonal.reshape(width)


def solution(mesh):
    placed = (P("row", "col", None, None), P("row", "col"), P(("row", "col"), None))
    return jax.shard_map(
        per_device,
        mesh=mesh,
        in_specs=placed,
        out_specs=(P(("row", "col"), None), P()),
        check_vma=False,
    )
```

```python
import functools
import math

import jax
import jax.numpy as jnp
from jax import lax
from jax.experimental import pallas as pl
from jax.experimental.pallas import tpu as pltpu
from jax.sharding import PartitionSpec as P

ITERS = 2
PANEL = 64
GROUP = 8
HIGH = lax.Precision.HIGHEST
ANY = pl.BlockSpec(memory_space=pl.ANY)
SMEM = pl.BlockSpec(memory_space=pltpu.SMEM)
VMEM = pl.BlockSpec(memory_space=pltpu.VMEM)
BIG = 60 * 2**20


def sort_kernel(cols, halves, slots, nb_ref, blk_ref, start_ref, *refs):
    outs, start_out = refs[: cols // 2], refs[cols // 2]
    held, rows, isem, osem = refs[cols // 2 + 1 :]
    half = held.shape[4]
    piece, width = start_ref.shape
    me = lax.axis_index("col")
    first = pltpu.make_async_copy(start_ref, rows.at[pl.ds(0, piece)], isem.at[cols * halves])
    first.start()
    ins = []
    for m in range(cols):
        to = jnp.bitwise_xor(me, m)
        for h in range(halves):
            at = to * halves + h
            ins.append(
                pltpu.make_async_copy(
                    blk_ref.at[at // 2, :, pl.ds(pl.multiple_of(at % 2 * half, half), half), :],
                    held.at[m // 2, m % 2, h],
                    isem.at[m * halves + h],
                )
            )
    for copy in ins:
        copy.start()
    lane = lax.broadcasted_iota(jnp.int32, (16, width), 1)
    numbers = jnp.zeros((16, width), jnp.float32)
    for i in range(halves * cols // 2):
        for n in range(slots):
            value = nb_ref[i, n].astype(jnp.float32)
            numbers = jnp.where(lane == i * slots + n, value, numbers)
    rows[piece:, :] = numbers.astype(rows.dtype)
    first.wait()
    copies = [pltpu.make_async_copy(rows, start_out, osem.at[cols // 2])]
    copies[0].start()
    for i in range(cols // 2):
        for copy in ins[2 * i * halves : 2 * (i + 1) * halves]:
            copy.wait()
        copies.append(pltpu.make_async_copy(held.at[i], outs[i], osem.at[i]))
        copies[-1].start()
    for copy in copies:
        copy.wait()


def sort_blocks(neighbours, blocks, start, cols):
    rows, slots, side, _ = blocks.shape
    halves = 2 * rows // cols
    piece, width = start.shape
    shape = (2, halves, slots, side // 2, side)
    return pl.pallas_call(
        functools.partial(sort_kernel, cols, halves, slots),
        out_shape=(jax.ShapeDtypeStruct(shape, blocks.dtype),) * (cols // 2)
        + (jax.ShapeDtypeStruct((piece + 16, width), start.dtype),),
        in_specs=[SMEM, ANY, ANY],
        out_specs=(ANY,) * (cols // 2 + 1),
        scratch_shapes=[
            pltpu.VMEM((cols // 2,) + shape, blocks.dtype),
            pltpu.VMEM((piece + 16, width), start.dtype),
            pltpu.SemaphoreType.DMA((cols * halves + 1,)),
            pltpu.SemaphoreType.DMA((cols // 2 + 1,)),
        ],
        compiler_params=pltpu.CompilerParams(vmem_limit_bytes=BIG),
        name="sort_blocks",
    )(neighbours, blocks, start)


def band_kernel(cols, first, *refs):
    known = not first
    held, refs = refs[:known], refs[known:]
    blks, owns, halos = refs[:cols], refs[cols : 2 * cols], refs[2 * cols : 3 * cols]
    keep_h, send_h, keep_o, send_o = refs[3 * cols : 3 * cols + 4]
    table, refs = (held if known else refs[3 * cols + 4 :])[0], refs[3 * cols + 4 + first :]
    blk, xwin, zacc, zbf, yref, nbf, nbi, nb_ref, isem, bsem, osem, nsem = refs
    piece, width = keep_h.shape[1:]
    _, halves, slots, half, side = blks[0].shape
    low = cols // 2 * piece
    me = lax.axis_index("col")
    odd = me % 2

    def own_at(c):
        return pl.multiple_of(low + c * piece, half)

    def halo_at(c):
        return pl.multiple_of(
            jnp.where(c < cols // 2, low + (cols + c) * piece, (c - cols // 2) * piece), half
        )

    xs, bs, ns = [], [], []
    if first:
        for m in range(cols):
            rows = owns[m].at[pl.ds(piece, 16)]
            ns.append(pltpu.make_async_copy(rows, nbf.at[m], nsem.at[m]))
            ns[m].start()
    for m in range(cols):
        c = jnp.bitwise_xor(me, m)
        for i, (src, at) in enumerate(((owns[m], own_at(c)), (halos[m], halo_at(c)))):
            xs.append(pltpu.make_async_copy(src.at[pl.ds(0, piece)], xwin.at[pl.ds(at, piece)], isem.at[2 * m + i]))
        bs.append(pltpu.make_async_copy(blks[m].at[m % 2], blk.at[m], bsem.at[m]))
    for copy in xs:
        copy.start()
    for copy in bs:
        copy.start()
    if first:
        for m in range(cols):
            ns[m].wait()
            nbi[m : m + 1, :] = nbf[m].astype(jnp.float32)[:1].astype(jnp.int32)
        written = pltpu.make_async_copy(nbi, table, nsem.at[0])
        written.start()
        written.wait()
    numbers = pltpu.make_async_copy(table, nb_ref, nsem.at[0])
    numbers.start()
    zacc[...] = jnp.zeros_like(zacc)
    numbers.wait()
    for copy in xs:
        copy.wait()

    single = 2 - 2 * odd
    pair_row = (me * halves + odd) // 2
    single_row = (me * halves + single) // 2

    def places(m, n):
        a = nb_ref[m, pair_row * slots + n] * side
        b = nb_ref[m, single_row * slots + n] * side
        return pl.multiple_of(a, side), pl.multiple_of(b, side)

    acc = jnp.zeros((2 * half, width), jnp.float32)
    acc1 = jnp.zeros((half, width), jnp.float32)
    for m in range(cols):
        bs[m].wait()
        for n in range(slots):
            a, b = places(m, n)
            pair = blk[m, pl.ds(odd, 2), n].reshape(2 * half, side)
            acc += jnp.dot(pair, xwin[pl.ds(a, side), :], preferred_element_type=jnp.float32)
            acc1 += jnp.dot(
                blk[m, single, n], xwin[pl.ds(b, side), :], preferred_element_type=jnp.float32
            )
    yref[: 2 * half] = acc.astype(jnp.bfloat16)
    yref[2 * half :] = acc1.astype(jnp.bfloat16)
    y = yref[: 2 * half]
    y1 = yref[2 * half :]
    turned = (((0,), (0,)), ((), ()))

    def back(m, carry):
        for n in range(slots):
            a, b = places(m, n)
            pair = blk[m, pl.ds(odd, 2), n].reshape(2 * half, side)
            zacc[pl.ds(a, side), :] += lax.dot_general(
                pair, y, turned, preferred_element_type=jnp.float32
            )
            zacc[pl.ds(b, side), :] += lax.dot_general(
                blk[m, single, n], y1, turned, preferred_element_type=jnp.float32
            )
        return carry

    lax.fori_loop(0, cols, back, 0, unroll=4)
    outs = []
    for refs2, at_of in (((keep_h, send_h), halo_at), ((keep_o, send_o), own_at)):
        for j in (1, 0):
            for i in range(cols // 2):
                at = at_of(jnp.bitwise_xor(me, 2 * i + j))
                zbf[pl.ds(at, piece), :] = zacc[pl.ds(at, piece), :].astype(jnp.bfloat16)
                copy = pltpu.make_async_copy(
                    zbf.at[pl.ds(at, piece)], refs2[j].at[i], osem.at[len(outs)]
                )
                copy.start()
                outs.append(copy)
    for copy in outs:
        copy.wait()


def band(table, blks, owns, halos):
    first = table is None
    cols = len(blks)
    _, halves, slots, half, side = blks[0].shape
    width = owns[0].shape[1]
    piece = halves * half
    window = 2 * cols * piece
    out = jax.ShapeDtypeStruct((cols // 2, piece, width), jnp.bfloat16)
    numbers = jax.ShapeDtypeStruct((cols, width), jnp.int32)
    results = pl.pallas_call(
        functools.partial(band_kernel, cols, first),
        out_shape=(out,) * 4 + (numbers,) * first,
        in_specs=[ANY] * (3 * cols + (not first)),
        out_specs=(ANY,) * (4 + first),
        scratch_shapes=[
            pltpu.VMEM((cols, halves, slots, half, side), jnp.bfloat16),
            pltpu.VMEM((window, width), jnp.bfloat16),
            pltpu.VMEM((window, width), jnp.float32),
            pltpu.VMEM((window, width), jnp.bfloat16),
            pltpu.VMEM((halves * half, width), jnp.bfloat16),
            pltpu.VMEM((cols, 16, width), jnp.bfloat16),
            pltpu.VMEM((cols, width), jnp.int32),
            pltpu.SMEM((cols, width), jnp.int32),
            pltpu.SemaphoreType.DMA((2 * cols,)),
            pltpu.SemaphoreType.DMA((cols,)),
            pltpu.SemaphoreType.DMA((2 * cols,)),
            pltpu.SemaphoreType.DMA((cols,)),
        ],
        compiler_params=pltpu.CompilerParams(vmem_limit_bytes=BIG),
        cost_estimate=pl.CostEstimate(
            flops=4 * cols * halves * slots * half * side * width,
            bytes_accessed=12 * 2**20,
            transcendentals=0,
        ),
        name="band",
    )(*(() if first else (table,)), *blks, *owns, *halos)
    return (results[4] if first else table), results[:4]


def gram_kernel(*refs):
    parts, (z_ref, g_ref) = refs[:-2], refs[-2:]
    z = parts[0][...]
    for part in parts[1:]:
        z = z + part[...].astype(jnp.float32)
    z_ref[...] = z
    g_ref[...] = lax.dot_general(
        z, z, (((0,), (0,)), ((), ())), precision=HIGH, preferred_element_type=jnp.float32
    )


def gram(*parts):
    shape = parts[0].shape
    return pl.pallas_call(
        gram_kernel,
        out_shape=(
            jax.ShapeDtypeStruct(shape, jnp.float32),
            jax.ShapeDtypeStruct((shape[1], shape[1]), jnp.float32),
        ),
        name="gram",
    )(*parts)


def panel(tiles, start, count):
    lanes = 128
    at, offset = start // lanes, start % lanes
    rows = lax.broadcasted_iota(jnp.int32, (count, lanes), 0)
    pivots = jnp.ones((count, lanes), jnp.float32)
    for k in range(0, count, GROUP):
        columns = [
            jnp.broadcast_to(
                tiles[at][:, offset + k + j : offset + k + j + 1], (count, lanes)
            )
            for j in range(GROUP)
        ]
        heads = [[t[k + j : k + j + 1, :] for t in tiles] for j in range(GROUP)]
        terms = []
        for j in range(GROUP):
            pivot = columns[j][k + j : k + j + 1, :]
            inverse = 1.0 / pivot
            scaled = [h * inverse for h in heads[j]]
            below = jnp.where(rows > k + j, columns[j], 0.0)
            terms.append((below, scaled))
            pivots = jnp.where(rows == k + j, pivot, pivots)
            for i in range(j + 1, GROUP):
                factor = columns[j][k + i : k + i + 1, :]
                columns[i] = columns[i] - columns[j] * (factor * inverse)
                heads[i] = [h - factor * s for h, s in zip(heads[i], scaled)]
        for t in range(len(tiles)):
            total = tiles[t]
            for below, scaled in terms:
                total = total - below * scaled[t]
            tiles[t] = total
    scale = 1.0 / jnp.sqrt(pivots)
    return [t * scale for t in tiles]


def orthonormal_kernel(factor, g_ref, z_ref, q_ref, d_ref, m):
    width = g_ref.shape[0]
    lanes = 128
    m[:, :width] = g_ref[...]
    r = lax.broadcasted_iota(jnp.int32, (width, width), 0)
    c = lax.broadcasted_iota(jnp.int32, (width, width), 1)
    eye = (r == c).astype(jnp.float32)
    m[:, width:] = eye
    for start in range(0, width, PANEL):
        end = start + PANEL
        first = start // lanes
        used = list(range(first, width // lanes)) + list(
            range(width // lanes, width // lanes + (end + lanes - 1) // lanes)
        )
        tiles = [m[start:end, t * lanes : (t + 1) * lanes] for t in used]
        tiles = panel(tiles, start - first * lanes, PANEL)
        for t, value in zip(used, tiles):
            m[start:end, t * lanes : (t + 1) * lanes] = value
        if end < width:
            upper = jnp.concatenate(tiles, axis=1)
            left = upper[:, : width - first * lanes]
            update = lax.dot_general(
                left, upper, (((0,), (0,)), ((), ())), precision=HIGH,
                preferred_element_type=jnp.float32,
            )
            skip = end - first * lanes
            for i, t in enumerate(used):
                m[end:, t * lanes : (t + 1) * lanes] -= update[skip:, i * lanes : (i + 1) * lanes]
    d_ref[...] = jnp.sum(m[:, :width] * eye, axis=0, keepdims=True)
    q = lax.dot_general(
        z_ref[...], m[:, width:], (((1,), (1,)), ((), ())), precision=HIGH,
        preferred_element_type=jnp.float32,
    )
    q_ref[...] = (q * factor).astype(q_ref.dtype)


def orthonormal(g, z, dtype, factor):
    width = z.shape[1]
    return pl.pallas_call(
        functools.partial(orthonormal_kernel, factor),
        out_shape=(
            jax.ShapeDtypeStruct(z.shape, dtype),
            jax.ShapeDtypeStruct((1, width), jnp.float32),
        ),
        scratch_shapes=[pltpu.VMEM((width, 2 * width), jnp.float32)],
        name="orthonormal",
    )(g, z)


def exchange(value, mask, axis):
    return lax.ppermute(value, axis, [(i, i ^ mask) for i in range(lax.axis_size(axis))])


def stages_of(count):
    if count == 32:
        return ((1, 2, 3), (4,), (8, 16, 24))
    return tuple((1 << i,) for i in range(count.bit_length() - 1))


def summed(value):
    cols = lax.axis_size("col")
    parts = lax.all_to_all(value, "col", 0, 0, tiled=True)
    part = jnp.sum(parts.reshape((cols, -1) + value.shape[1:]), axis=0)
    for stage in stages_of(lax.axis_size("row")):
        others = [exchange(part, mask, "row") for mask in stage]
        part = part + others[0]
        if len(others) == 3:
            part = part + (others[1] + others[2])
    return lax.all_to_all(jnp.tile(part, (cols, 1)), "col", 0, 0, tiled=True)


def per_device(blocks, neighbours, start):
    cols = lax.axis_size("col")
    groups = lax.axis_size("row")
    piece, width = start.shape
    total_rows = piece * cols * groups
    chips = range(0, cols, 2)

    def hops(sign):
        pairs = []
        for g in range(groups):
            for c in range(cols):
                step = -sign if c < cols // 2 else sign
                pairs.append((g * cols + c, (g + step) % groups * cols + c))
        return pairs

    near, far = hops(1), hops(-1)

    def to_group(value, pairs):
        return lax.ppermute(value, ("row", "col"), pairs)

    *sorted_blocks, current = sort_blocks(neighbours, blocks, start, cols)
    blks = []
    for m in chips:
        got = exchange(sorted_blocks[m // 2], m, "col") if m else sorted_blocks[0]
        blks += [got, exchange(got, 1, "col")]
    table = None
    for step in range(ITERS):
        own_chips = {m: exchange(current, m, "col") if m else current for m in chips}
        halo_chips = {m: to_group(own_chips[m], near if m < cols // 2 else far) for m in chips}
        owns, halos = [], []
        for m in chips:
            owns += [own_chips[m], exchange(own_chips[m], 1, "col")]
        for m in chips:
            halos += [halo_chips[m], exchange(halo_chips[m], 1, "col")]
        table, (keep_h, send_h, keep_o, send_o) = band(table, blks, owns, halos)

        def folded(keep, send):
            got = exchange(send, 1, "col")
            sums = [keep[i].astype(jnp.float32) + got[i].astype(jnp.float32) for i in range(cols // 2)]
            return [sums[0]] + [
                exchange(sums[m // 2].astype(jnp.bfloat16), m, "col") for m in chips if m
            ]

        halo_parts = folded(keep_h, send_h)
        halo_sum = halo_parts[0]
        for part in halo_parts[1:]:
            halo_sum = halo_sum + part.astype(jnp.float32)
        returned = to_group(halo_sum.astype(jnp.bfloat16), far)
        z, local = gram(*folded(keep_o, send_o), returned)
        g = summed(local)
        last = step == ITERS - 1
        current, diagonal = orthonormal(
            g, z, jnp.float32 if last else jnp.bfloat16, math.sqrt(total_rows) if last else 1.0
        )
    return current, diagonal.reshape(width)


def solution(mesh):
    placed = (P("row", "col", None, None), P("row", "col"), P(("row", "col"), None))
    return jax.shard_map(
        per_device,
        mesh=mesh,
        in_specs=placed,
        out_specs=(P(("row", "col"), None), P()),
        check_vma=False,
    )
```

```python
import functools
import math

import jax
import jax.numpy as jnp
from jax import lax
from jax.experimental import pallas as pl
from jax.experimental.pallas import tpu as pltpu
from jax.sharding import PartitionSpec as P

ITERS = 2
PANEL = 64
GROUP = 8
HIGH = lax.Precision.HIGHEST
ANY = pl.BlockSpec(memory_space=pl.ANY)
SMEM = pl.BlockSpec(memory_space=pltpu.SMEM)
VMEM = pl.BlockSpec(memory_space=pltpu.VMEM)
BIG = 60 * 2**20


def sort_kernel(cols, halves, slots, nb_ref, blk_ref, start_ref, *refs):
    outs, start_out = refs[: cols // 2], refs[cols // 2]
    held, rows, isem, osem = refs[cols // 2 + 1 :]
    half = held.shape[4]
    piece, width = start_ref.shape
    me = lax.axis_index("col")
    first = pltpu.make_async_copy(start_ref, rows.at[pl.ds(0, piece)], isem.at[cols * halves])
    first.start()
    ins = []
    for m in range(cols):
        to = jnp.bitwise_xor(me, m)
        for h in range(halves):
            at = to * halves + h
            ins.append(
                pltpu.make_async_copy(
                    blk_ref.at[at // 2, :, pl.ds(pl.multiple_of(at % 2 * half, half), half), :],
                    held.at[m // 2, m % 2, h],
                    isem.at[m * halves + h],
                )
            )
    for copy in ins:
        copy.start()
    lane = lax.broadcasted_iota(jnp.int32, (16, width), 1)
    numbers = jnp.zeros((16, width), jnp.float32)
    for i in range(halves * cols // 2):
        for n in range(slots):
            value = nb_ref[i, n].astype(jnp.float32)
            numbers = jnp.where(lane == i * slots + n, value, numbers)
    rows[piece:, :] = numbers.astype(rows.dtype)
    first.wait()
    copies = [pltpu.make_async_copy(rows, start_out, osem.at[cols // 2])]
    copies[0].start()
    for i in range(cols // 2):
        for copy in ins[2 * i * halves : 2 * (i + 1) * halves]:
            copy.wait()
        copies.append(pltpu.make_async_copy(held.at[i], outs[i], osem.at[i]))
        copies[-1].start()
    for copy in copies:
        copy.wait()


def sort_blocks(neighbours, blocks, start, cols):
    rows, slots, side, _ = blocks.shape
    halves = 2 * rows // cols
    piece, width = start.shape
    shape = (2, halves, slots, side // 2, side)
    return pl.pallas_call(
        functools.partial(sort_kernel, cols, halves, slots),
        out_shape=(jax.ShapeDtypeStruct(shape, blocks.dtype),) * (cols // 2)
        + (jax.ShapeDtypeStruct((piece + 16, width), start.dtype),),
        in_specs=[SMEM, ANY, ANY],
        out_specs=(ANY,) * (cols // 2 + 1),
        scratch_shapes=[
            pltpu.VMEM((cols // 2,) + shape, blocks.dtype),
            pltpu.VMEM((piece + 16, width), start.dtype),
            pltpu.SemaphoreType.DMA((cols * halves + 1,)),
            pltpu.SemaphoreType.DMA((cols // 2 + 1,)),
        ],
        compiler_params=pltpu.CompilerParams(vmem_limit_bytes=BIG),
        name="sort_blocks",
    )(neighbours, blocks, start)


def band_kernel(cols, first, *refs):
    known = not first
    held, refs = refs[:known], refs[known:]
    blks, owns, halos = refs[:cols], refs[cols : 2 * cols], refs[2 * cols : 3 * cols]
    keep_h, send_h, keep_o, send_o = refs[3 * cols : 3 * cols + 4]
    table, refs = (held if known else refs[3 * cols + 4 :])[0], refs[3 * cols + 4 + first :]
    blk, xwin, zacc, zbf, yref, nbf, nbi, nb_ref, isem, bsem, osem, nsem = refs
    piece, width = keep_h.shape[1:]
    _, halves, slots, half, side = blks[0].shape
    low = cols // 2 * piece
    me = lax.axis_index("col")
    odd = me % 2

    def own_at(c):
        return pl.multiple_of(low + c * piece, half)

    def halo_at(c):
        return pl.multiple_of(
            jnp.where(c < cols // 2, low + (cols + c) * piece, (c - cols // 2) * piece), half
        )

    xs, bs, ns = [], [], []
    if first:
        for m in range(cols):
            rows = owns[m].at[pl.ds(piece, 16)]
            ns.append(pltpu.make_async_copy(rows, nbf.at[m], nsem.at[m]))
            ns[m].start()
    for m in range(cols):
        c = jnp.bitwise_xor(me, m)
        for i, (src, at) in enumerate(((owns[m], own_at(c)), (halos[m], halo_at(c)))):
            xs.append(pltpu.make_async_copy(src.at[pl.ds(0, piece)], xwin.at[pl.ds(at, piece)], isem.at[2 * m + i]))
        bs.append(pltpu.make_async_copy(blks[m].at[m % 2], blk.at[m], bsem.at[m]))
    for copy in xs:
        copy.start()
    for copy in bs:
        copy.start()
    if first:
        for m in range(cols):
            ns[m].wait()
            nbi[m : m + 1, :] = nbf[m].astype(jnp.float32)[:1].astype(jnp.int32)
        written = pltpu.make_async_copy(nbi, table, nsem.at[0])
        written.start()
        written.wait()
    numbers = pltpu.make_async_copy(table, nb_ref, nsem.at[0])
    numbers.start()
    zacc[...] = jnp.zeros_like(zacc)
    numbers.wait()
    for copy in xs:
        copy.wait()

    single = 2 - 2 * odd
    pair_row = (me * halves + odd) // 2
    single_row = (me * halves + single) // 2

    def places(m, n):
        a = nb_ref[m, pair_row * slots + n] * side
        b = nb_ref[m, single_row * slots + n] * side
        return pl.multiple_of(a, side), pl.multiple_of(b, side)

    acc = jnp.zeros((2 * half, width), jnp.float32)
    acc1 = jnp.zeros((half, width), jnp.float32)
    for m in range(cols):
        bs[m].wait()
        for n in range(slots):
            a, b = places(m, n)
            pair = blk[m, pl.ds(odd, 2), n].reshape(2 * half, side)
            acc += jnp.dot(pair, xwin[pl.ds(a, side), :], preferred_element_type=jnp.float32)
            acc1 += jnp.dot(
                blk[m, single, n], xwin[pl.ds(b, side), :], preferred_element_type=jnp.float32
            )
    yref[: 2 * half] = acc.astype(jnp.bfloat16)
    yref[2 * half :] = acc1.astype(jnp.bfloat16)
    y = yref[: 2 * half]
    y1 = yref[2 * half :]
    turned = (((0,), (0,)), ((), ()))

    def back(m, carry):
        for n in range(slots):
            a, b = places(m, n)
            pair = blk[m, pl.ds(odd, 2), n].reshape(2 * half, side)
            zacc[pl.ds(a, side), :] += lax.dot_general(
                pair, y, turned, preferred_element_type=jnp.float32
            )
            zacc[pl.ds(b, side), :] += lax.dot_general(
                blk[m, single, n], y1, turned, preferred_element_type=jnp.float32
            )
        return carry

    lax.fori_loop(0, cols, back, 0, unroll=4)
    outs = []
    for refs2, at_of in (((keep_h, send_h), halo_at), ((keep_o, send_o), own_at)):
        for j in (1, 0):
            for i in range(cols // 2):
                at = at_of(jnp.bitwise_xor(me, 2 * i + j))
                zbf[pl.ds(at, piece), :] = zacc[pl.ds(at, piece), :].astype(jnp.bfloat16)
                copy = pltpu.make_async_copy(
                    zbf.at[pl.ds(at, piece)], refs2[j].at[i], osem.at[len(outs)]
                )
                copy.start()
                outs.append(copy)
    for copy in outs:
        copy.wait()


def band(table, blks, owns, halos):
    first = table is None
    cols = len(blks)
    _, halves, slots, half, side = blks[0].shape
    width = owns[0].shape[1]
    piece = halves * half
    window = 2 * cols * piece
    out = jax.ShapeDtypeStruct((cols // 2, piece, width), jnp.bfloat16)
    numbers = jax.ShapeDtypeStruct((cols, width), jnp.int32)
    results = pl.pallas_call(
        functools.partial(band_kernel, cols, first),
        out_shape=(out,) * 4 + (numbers,) * first,
        in_specs=[ANY] * (3 * cols + (not first)),
        out_specs=(ANY,) * (4 + first),
        scratch_shapes=[
            pltpu.VMEM((cols, halves, slots, half, side), jnp.bfloat16),
            pltpu.VMEM((window, width), jnp.bfloat16),
            pltpu.VMEM((window, width), jnp.float32),
            pltpu.VMEM((window, width), jnp.bfloat16),
            pltpu.VMEM((halves * half, width), jnp.bfloat16),
            pltpu.VMEM((cols, 16, width), jnp.bfloat16),
            pltpu.VMEM((cols, width), jnp.int32),
            pltpu.SMEM((cols, width), jnp.int32),
            pltpu.SemaphoreType.DMA((2 * cols,)),
            pltpu.SemaphoreType.DMA((cols,)),
            pltpu.SemaphoreType.DMA((2 * cols,)),
            pltpu.SemaphoreType.DMA((cols,)),
        ],
        compiler_params=pltpu.CompilerParams(vmem_limit_bytes=BIG),
        cost_estimate=pl.CostEstimate(
            flops=4 * cols * halves * slots * half * side * width,
            bytes_accessed=12 * 2**20,
            transcendentals=0,
        ),
        name="band",
    )(*(() if first else (table,)), *blks, *owns, *halos)
    return (results[4] if first else table), results[:4]


def gram_kernel(*refs):
    parts, (z_ref, g_ref) = refs[:-2], refs[-2:]
    z = parts[0][...]
    for part in parts[1:]:
        z = z + part[...].astype(jnp.float32)
    z_ref[...] = z
    g_ref[...] = lax.dot_general(
        z, z, (((0,), (0,)), ((), ())), precision=HIGH, preferred_element_type=jnp.float32
    )


def gram(*parts):
    shape = parts[0].shape
    return pl.pallas_call(
        gram_kernel,
        out_shape=(
            jax.ShapeDtypeStruct(shape, jnp.float32),
            jax.ShapeDtypeStruct((shape[1], shape[1]), jnp.float32),
        ),
        name="gram",
    )(*parts)


def panel(tiles, start, count):
    lanes = 128
    at, offset = start // lanes, start % lanes
    rows = lax.broadcasted_iota(jnp.int32, (count, lanes), 0)
    pivots = jnp.ones((count, lanes), jnp.float32)
    for k in range(0, count, GROUP):
        columns = [
            jnp.broadcast_to(
                tiles[at][:, offset + k + j : offset + k + j + 1], (count, lanes)
            )
            for j in range(GROUP)
        ]
        heads = [[t[k + j : k + j + 1, :] for t in tiles] for j in range(GROUP)]
        terms = []
        for j in range(GROUP):
            pivot = columns[j][k + j : k + j + 1, :]
            inverse = 1.0 / pivot
            scaled = [h * inverse for h in heads[j]]
            below = jnp.where(rows > k + j, columns[j], 0.0)
            terms.append((below, scaled))
            pivots = jnp.where(rows == k + j, pivot, pivots)
            for i in range(j + 1, GROUP):
                factor = columns[j][k + i : k + i + 1, :]
                columns[i] = columns[i] - columns[j] * (factor * inverse)
                heads[i] = [h - factor * s for h, s in zip(heads[i], scaled)]
        for t in range(len(tiles)):
            total = tiles[t]
            for below, scaled in terms:
                total = total - below * scaled[t]
            tiles[t] = total
    scale = 1.0 / jnp.sqrt(pivots)
    return [t * scale for t in tiles]


def orthonormal_kernel(factor, g_ref, z_ref, q_ref, d_ref, m):
    width = g_ref.shape[0]
    lanes = 128
    m[:, :width] = g_ref[...]
    r = lax.broadcasted_iota(jnp.int32, (width, width), 0)
    c = lax.broadcasted_iota(jnp.int32, (width, width), 1)
    eye = (r == c).astype(jnp.float32)
    m[:, width:] = eye
    for start in range(0, width, PANEL):
        end = start + PANEL
        first = start // lanes
        used = list(range(first, width // lanes)) + list(
            range(width // lanes, width // lanes + (end + lanes - 1) // lanes)
        )
        tiles = [m[start:end, t * lanes : (t + 1) * lanes] for t in used]
        tiles = panel(tiles, start - first * lanes, PANEL)
        for t, value in zip(used, tiles):
            m[start:end, t * lanes : (t + 1) * lanes] = value
        if end < width:
            upper = jnp.concatenate(tiles, axis=1)
            left = upper[:, : width - first * lanes]
            update = lax.dot_general(
                left, upper, (((0,), (0,)), ((), ())), precision=HIGH,
                preferred_element_type=jnp.float32,
            )
            skip = end - first * lanes
            for i, t in enumerate(used):
                m[end:, t * lanes : (t + 1) * lanes] -= update[skip:, i * lanes : (i + 1) * lanes]
    d_ref[...] = jnp.sum(m[:, :width] * eye, axis=0, keepdims=True)
    q = lax.dot_general(
        z_ref[...], m[:, width:], (((1,), (1,)), ((), ())), precision=HIGH,
        preferred_element_type=jnp.float32,
    )
    q_ref[...] = (q * factor).astype(q_ref.dtype)


def orthonormal(g, z, dtype, factor):
    width = z.shape[1]
    return pl.pallas_call(
        functools.partial(orthonormal_kernel, factor),
        out_shape=(
            jax.ShapeDtypeStruct(z.shape, dtype),
            jax.ShapeDtypeStruct((1, width), jnp.float32),
        ),
        scratch_shapes=[pltpu.VMEM((width, 2 * width), jnp.float32)],
        name="orthonormal",
    )(g, z)


def exchange(value, mask, axis):
    return lax.ppermute(value, axis, [(i, i ^ mask) for i in range(lax.axis_size(axis))])


def stages_of(count):
    if count == 32:
        return ((1, 2, 3), (4,), (8, 16, 24))
    return tuple((1 << i,) for i in range(count.bit_length() - 1))


def summed(value):
    cols = lax.axis_size("col")
    parts = lax.all_to_all(value, "col", 0, 0, tiled=True)
    part = jnp.sum(parts.reshape((cols, -1) + value.shape[1:]), axis=0)
    for stage in stages_of(lax.axis_size("row")):
        others = [exchange(part, mask, "row") for mask in stage]
        part = part + others[0]
        if len(others) == 3:
            part = part + (others[1] + others[2])
    return lax.all_to_all(jnp.tile(part, (cols, 1)), "col", 0, 0, tiled=True)


def per_device(blocks, neighbours, start):
    cols = lax.axis_size("col")
    groups = lax.axis_size("row")
    piece, width = start.shape
    total_rows = piece * cols * groups
    chips = range(0, cols, 2)

    def step_of(c):
        return -1 if c < cols // 2 else 1

    def across(value, m, back=False):
        pairs = [
            (g * cols + c, (g + step_of(c)) % groups * cols + (c ^ m))
            for g in range(groups)
            for c in range(cols)
        ]
        return lax.ppermute(value, ("row", "col"), [(b, a) for a, b in pairs] if back else pairs)

    def along(value, m):
        pairs = [
            (g * cols + c, (g + step_of(c ^ m)) % groups * cols + c)
            for g in range(groups)
            for c in range(cols)
        ]
        return lax.ppermute(value, ("row", "col"), pairs)

    *sorted_blocks, current = sort_blocks(neighbours, blocks, start, cols)
    blks = []
    for m in chips:
        got = exchange(sorted_blocks[m // 2], m, "col") if m else sorted_blocks[0]
        blks += [got, exchange(got, 1, "col")]
    table = None
    for step in range(ITERS):
        own_chips = {m: exchange(current, m, "col") if m else current for m in chips}
        if step == 0:
            halo_chips = {m: along(own_chips[m], m) for m in chips}
        else:
            halo_chips = {m: across(current, m) for m in chips}
        owns, halos = [], []
        for m in chips:
            owns += [own_chips[m], exchange(own_chips[m], 1, "col")]
        for m in chips:
            halos += [halo_chips[m], exchange(halo_chips[m], 1, "col")]
        table, (keep_h, send_h, keep_o, send_o) = band(table, blks, owns, halos)

        def chip_sum(keep, send):
            got = exchange(send, 1, "col")
            return [keep[i].astype(jnp.float32) + got[i].astype(jnp.float32) for i in range(cols // 2)]

        halo_terms = chip_sum(keep_h, send_h)
        returned = [across(halo_terms[m // 2].astype(jnp.bfloat16), m, True) for m in chips]
        own_terms = chip_sum(keep_o, send_o)
        others = [exchange(own_terms[m // 2].astype(jnp.bfloat16), m, "col") for m in chips if m]
        z, local = gram(own_terms[0], *others, *returned)
        g = summed(local)
        last = step == ITERS - 1
        current, diagonal = orthonormal(
            g, z, jnp.float32 if last else jnp.bfloat16, math.sqrt(total_rows) if last else 1.0
        )
    return current, diagonal.reshape(width)


def solution(mesh):
    placed = (P("row", "col", None, None), P("row", "col"), P(("row", "col"), None))
    return jax.shard_map(
        per_device,
        mesh=mesh,
        in_specs=placed,
        out_specs=(P(("row", "col"), None), P()),
        check_vma=False,
    )
```

```python
import functools
import math

import jax
import jax.numpy as jnp
from jax import lax
from jax.experimental import pallas as pl
from jax.experimental.pallas import tpu as pltpu
from jax.sharding import PartitionSpec as P

ITERS = 2
PANEL = 64
GROUP = 8
HIGH = lax.Precision.HIGHEST
ANY = pl.BlockSpec(memory_space=pl.ANY)
SMEM = pl.BlockSpec(memory_space=pltpu.SMEM)
VMEM = pl.BlockSpec(memory_space=pltpu.VMEM)
BIG = 60 * 2**20


def sort_kernel(cols, halves, slots, nb_ref, blk_ref, start_ref, *refs):
    outs, start_out = refs[: cols // 2], refs[cols // 2]
    held, rows, isem, osem = refs[cols // 2 + 1 :]
    half = held.shape[4]
    piece, width = start_ref.shape
    me = lax.axis_index("col")
    first = pltpu.make_async_copy(start_ref, rows.at[pl.ds(0, piece)], isem.at[cols * halves])
    first.start()
    ins = []
    for m in range(cols):
        to = jnp.bitwise_xor(me, m)
        for h in range(halves):
            at = to * halves + h
            ins.append(
                pltpu.make_async_copy(
                    blk_ref.at[at // 2, :, pl.ds(pl.multiple_of(at % 2 * half, half), half), :],
                    held.at[m // 2, m % 2, h],
                    isem.at[m * halves + h],
                )
            )
    for copy in ins:
        copy.start()
    lane = lax.broadcasted_iota(jnp.int32, (16, width), 1)
    numbers = jnp.zeros((16, width), jnp.float32)
    for i in range(halves * cols // 2):
        for n in range(slots):
            value = nb_ref[i, n].astype(jnp.float32)
            numbers = jnp.where(lane == i * slots + n, value, numbers)
    rows[piece:, :] = numbers.astype(rows.dtype)
    first.wait()
    copies = [pltpu.make_async_copy(rows, start_out, osem.at[cols // 2])]
    copies[0].start()
    for i in range(cols // 2):
        for copy in ins[2 * i * halves : 2 * (i + 1) * halves]:
            copy.wait()
        copies.append(pltpu.make_async_copy(held.at[i], outs[i], osem.at[i]))
        copies[-1].start()
    for copy in copies:
        copy.wait()


def sort_blocks(neighbours, blocks, start, cols):
    rows, slots, side, _ = blocks.shape
    halves = 2 * rows // cols
    piece, width = start.shape
    shape = (2, halves, slots, side // 2, side)
    return pl.pallas_call(
        functools.partial(sort_kernel, cols, halves, slots),
        out_shape=(jax.ShapeDtypeStruct(shape, blocks.dtype),) * (cols // 2)
        + (jax.ShapeDtypeStruct((piece + 16, width), start.dtype),),
        in_specs=[SMEM, ANY, ANY],
        out_specs=(ANY,) * (cols // 2 + 1),
        scratch_shapes=[
            pltpu.VMEM((cols // 2,) + shape, blocks.dtype),
            pltpu.VMEM((piece + 16, width), start.dtype),
            pltpu.SemaphoreType.DMA((cols * halves + 1,)),
            pltpu.SemaphoreType.DMA((cols // 2 + 1,)),
        ],
        compiler_params=pltpu.CompilerParams(vmem_limit_bytes=BIG),
        name="sort_blocks",
    )(neighbours, blocks, start)


def band_kernel(cols, first, *refs):
    known = not first
    held, refs = refs[:known], refs[known:]
    blks, owns, halos = refs[:cols], refs[cols : 2 * cols], refs[2 * cols : 3 * cols]
    keep_h, send_h, keep_o, send_o = refs[3 * cols : 3 * cols + 4]
    table, refs = (held if known else refs[3 * cols + 4 :])[0], refs[3 * cols + 4 + first :]
    blk, xwin, zacc, zbf, yref, nbf, nbi, nb_ref, isem, bsem, osem, nsem = refs
    piece, width = keep_h.shape[1:]
    _, halves, slots, half, side = blks[0].shape
    low = cols // 2 * piece
    me = lax.axis_index("col")
    odd = me % 2

    def own_at(c):
        return pl.multiple_of(low + c * piece, half)

    def halo_at(c):
        return pl.multiple_of(
            jnp.where(c < cols // 2, low + (cols + c) * piece, (c - cols // 2) * piece), half
        )

    xs, bs, ns = [], [], []
    if first:
        for m in range(cols):
            rows = owns[m].at[pl.ds(piece, 16)]
            ns.append(pltpu.make_async_copy(rows, nbf.at[m], nsem.at[m]))
            ns[m].start()
    for m in range(cols):
        c = jnp.bitwise_xor(me, m)
        for i, (src, at) in enumerate(((owns[m], own_at(c)), (halos[m], halo_at(c)))):
            xs.append(pltpu.make_async_copy(src.at[pl.ds(0, piece)], xwin.at[pl.ds(at, piece)], isem.at[2 * m + i]))
        bs.append(pltpu.make_async_copy(blks[m].at[m % 2], blk.at[m], bsem.at[m]))
    for copy in xs:
        copy.start()
    for copy in bs:
        copy.start()
    if first:
        for m in range(cols):
            ns[m].wait()
            nbi[m : m + 1, :] = nbf[m].astype(jnp.float32)[:1].astype(jnp.int32)
        written = pltpu.make_async_copy(nbi, table, nsem.at[0])
        written.start()
        written.wait()
    numbers = pltpu.make_async_copy(table, nb_ref, nsem.at[0])
    numbers.start()
    zacc[...] = jnp.zeros_like(zacc)
    numbers.wait()
    for copy in xs:
        copy.wait()

    single = 2 - 2 * odd
    pair_row = (me * halves + odd) // 2
    single_row = (me * halves + single) // 2

    def places(m, n):
        a = nb_ref[m, pair_row * slots + n] * side
        b = nb_ref[m, single_row * slots + n] * side
        return pl.multiple_of(a, side), pl.multiple_of(b, side)

    acc = jnp.zeros((2 * half, width), jnp.float32)
    acc1 = jnp.zeros((half, width), jnp.float32)
    for m in range(cols):
        bs[m].wait()
        for n in range(slots):
            a, b = places(m, n)
            pair = blk[m, pl.ds(odd, 2), n].reshape(2 * half, side)
            acc += jnp.dot(pair, xwin[pl.ds(a, side), :], preferred_element_type=jnp.float32)
            acc1 += jnp.dot(
                blk[m, single, n], xwin[pl.ds(b, side), :], preferred_element_type=jnp.float32
            )
    yref[: 2 * half] = acc.astype(jnp.bfloat16)
    yref[2 * half :] = acc1.astype(jnp.bfloat16)
    y = yref[: 2 * half]
    y1 = yref[2 * half :]
    turned = (((0,), (0,)), ((), ()))

    def back(m, carry):
        for n in range(slots):
            a, b = places(m, n)
            pair = blk[m, pl.ds(odd, 2), n].reshape(2 * half, side)
            zacc[pl.ds(a, side), :] += lax.dot_general(
                pair, y, turned, preferred_element_type=jnp.float32
            )
            zacc[pl.ds(b, side), :] += lax.dot_general(
                blk[m, single, n], y1, turned, preferred_element_type=jnp.float32
            )
        return carry

    lax.fori_loop(0, cols, back, 0, unroll=4)
    outs = []
    for refs2, at_of in (((keep_h, send_h), halo_at), ((keep_o, send_o), own_at)):
        for j in (1, 0):
            for i in range(cols // 2):
                at = at_of(jnp.bitwise_xor(me, 2 * i + j))
                zbf[pl.ds(at, piece), :] = zacc[pl.ds(at, piece), :].astype(jnp.bfloat16)
                copy = pltpu.make_async_copy(
                    zbf.at[pl.ds(at, piece)], refs2[j].at[i], osem.at[len(outs)]
                )
                copy.start()
                outs.append(copy)
    for copy in outs:
        copy.wait()


def band(table, blks, owns, halos):
    first = table is None
    cols = len(blks)
    _, halves, slots, half, side = blks[0].shape
    width = owns[0].shape[1]
    piece = halves * half
    window = 2 * cols * piece
    out = jax.ShapeDtypeStruct((cols // 2, piece, width), jnp.bfloat16)
    numbers = jax.ShapeDtypeStruct((cols, width), jnp.int32)
    results = pl.pallas_call(
        functools.partial(band_kernel, cols, first),
        out_shape=(out,) * 4 + (numbers,) * first,
        in_specs=[ANY] * (3 * cols + (not first)),
        out_specs=(ANY,) * (4 + first),
        scratch_shapes=[
            pltpu.VMEM((cols, halves, slots, half, side), jnp.bfloat16),
            pltpu.VMEM((window, width), jnp.bfloat16),
            pltpu.VMEM((window, width), jnp.float32),
            pltpu.VMEM((window, width), jnp.bfloat16),
            pltpu.VMEM((halves * half, width), jnp.bfloat16),
            pltpu.VMEM((cols, 16, width), jnp.bfloat16),
            pltpu.VMEM((cols, width), jnp.int32),
            pltpu.SMEM((cols, width), jnp.int32),
            pltpu.SemaphoreType.DMA((2 * cols,)),
            pltpu.SemaphoreType.DMA((cols,)),
            pltpu.SemaphoreType.DMA((2 * cols,)),
            pltpu.SemaphoreType.DMA((cols,)),
        ],
        compiler_params=pltpu.CompilerParams(vmem_limit_bytes=BIG),
        cost_estimate=pl.CostEstimate(
            flops=4 * cols * halves * slots * half * side * width,
            bytes_accessed=12 * 2**20,
            transcendentals=0,
        ),
        name="band",
    )(*(() if first else (table,)), *blks, *owns, *halos)
    return (results[4] if first else table), results[:4]


def gram_kernel(*refs):
    parts, (z_ref, keep_ref, send_ref, g) = refs[:-4], refs[-4:]
    z = parts[0][...]
    for part in parts[1:]:
        z = z + part[...].astype(jnp.float32)
    z_ref[...] = z
    g[...] = lax.dot_general(
        z, z, (((0,), (0,)), ((), ())), precision=HIGH, preferred_element_type=jnp.float32
    )
    me = lax.axis_index("col")
    chips, rows, _ = keep_ref.shape
    for i in range(chips):
        for j, out in ((0, keep_ref), (1, send_ref)):
            at = pl.multiple_of(jnp.bitwise_xor(me, 2 * i + j) * rows, rows)
            out[i] = g[pl.ds(at, rows), :]


def gram(cols, *parts):
    shape = parts[0].shape
    width = shape[1]
    half = jax.ShapeDtypeStruct((cols // 2, width // cols, width), jnp.float32)
    return pl.pallas_call(
        gram_kernel,
        out_shape=(jax.ShapeDtypeStruct(shape, jnp.float32), half, half),
        scratch_shapes=[pltpu.VMEM((width, width), jnp.float32)],
        name="gram",
    )(*parts)


def panel(tiles, start, count):
    lanes = 128
    at, offset = start // lanes, start % lanes
    rows = lax.broadcasted_iota(jnp.int32, (count, lanes), 0)
    pivots = jnp.ones((count, lanes), jnp.float32)
    for k in range(0, count, GROUP):
        columns = [
            jnp.broadcast_to(
                tiles[at][:, offset + k + j : offset + k + j + 1], (count, lanes)
            )
            for j in range(GROUP)
        ]
        heads = [[t[k + j : k + j + 1, :] for t in tiles] for j in range(GROUP)]
        terms = []
        for j in range(GROUP):
            pivot = columns[j][k + j : k + j + 1, :]
            inverse = 1.0 / pivot
            scaled = [h * inverse for h in heads[j]]
            below = jnp.where(rows > k + j, columns[j], 0.0)
            terms.append((below, scaled))
            pivots = jnp.where(rows == k + j, pivot, pivots)
            for i in range(j + 1, GROUP):
                factor = columns[j][k + i : k + i + 1, :]
                columns[i] = columns[i] - columns[j] * (factor * inverse)
                heads[i] = [h - factor * s for h, s in zip(heads[i], scaled)]
        for t in range(len(tiles)):
            total = tiles[t]
            for below, scaled in terms:
                total = total - below * scaled[t]
            tiles[t] = total
    scale = 1.0 / jnp.sqrt(pivots)
    return [t * scale for t in tiles]


def orthonormal_kernel(factor, *refs):
    parts, (z_ref, q_ref, d_ref, m) = refs[:-4], refs[-4:]
    rows, width = parts[0].shape
    lanes = 128
    me = lax.axis_index("col")
    for i, part in enumerate(parts):
        at = pl.multiple_of(jnp.bitwise_xor(me, i) * rows, rows)
        m[pl.ds(at, rows), :width] = part[...]
    r = lax.broadcasted_iota(jnp.int32, (width, width), 0)
    c = lax.broadcasted_iota(jnp.int32, (width, width), 1)
    eye = (r == c).astype(jnp.float32)
    m[:, width:] = eye
    for start in range(0, width, PANEL):
        end = start + PANEL
        first = start // lanes
        used = list(range(first, width // lanes)) + list(
            range(width // lanes, width // lanes + (end + lanes - 1) // lanes)
        )
        tiles = [m[start:end, t * lanes : (t + 1) * lanes] for t in used]
        tiles = panel(tiles, start - first * lanes, PANEL)
        for t, value in zip(used, tiles):
            m[start:end, t * lanes : (t + 1) * lanes] = value
        if end < width:
            upper = jnp.concatenate(tiles, axis=1)
            left = upper[:, : width - first * lanes]
            update = lax.dot_general(
                left, upper, (((0,), (0,)), ((), ())), precision=HIGH,
                preferred_element_type=jnp.float32,
            )
            skip = end - first * lanes
            for i, t in enumerate(used):
                m[end:, t * lanes : (t + 1) * lanes] -= update[skip:, i * lanes : (i + 1) * lanes]
    d_ref[...] = jnp.sum(m[:, :width] * eye, axis=0, keepdims=True)
    q = lax.dot_general(
        z_ref[...], m[:, width:], (((1,), (1,)), ((), ())), precision=HIGH,
        preferred_element_type=jnp.float32,
    )
    q_ref[...] = (q * factor).astype(q_ref.dtype)


def orthonormal(parts, z, dtype, factor):
    width = z.shape[1]
    return pl.pallas_call(
        functools.partial(orthonormal_kernel, factor),
        out_shape=(
            jax.ShapeDtypeStruct(z.shape, dtype),
            jax.ShapeDtypeStruct((1, width), jnp.float32),
        ),
        scratch_shapes=[pltpu.VMEM((width, 2 * width), jnp.float32)],
        name="orthonormal",
    )(*parts, z)


def exchange(value, mask, axis):
    return lax.ppermute(value, axis, [(i, i ^ mask) for i in range(lax.axis_size(axis))])


def stages_of(count):
    if count == 32:
        return ((1, 2, 3), (4,), (8, 16, 24))
    return tuple((1 << i,) for i in range(count.bit_length() - 1))


def summed(keep, send):
    chips = keep.shape[0]
    got = exchange(send, 1, "col")
    sums = [keep[i] + got[i] for i in range(chips)]
    part = sums[0]
    for i in range(1, chips):
        part = part + exchange(sums[i], 2 * i, "col")
    for stage in stages_of(lax.axis_size("row")):
        others = [exchange(part, mask, "row") for mask in stage]
        part = part + others[0]
        if len(others) == 3:
            part = part + (others[1] + others[2])
    out = []
    for i in range(chips):
        rows = exchange(part, 2 * i, "col") if i else part
        out += [rows, exchange(rows, 1, "col")]
    return out


def per_device(blocks, neighbours, start):
    cols = lax.axis_size("col")
    groups = lax.axis_size("row")
    piece, width = start.shape
    total_rows = piece * cols * groups
    chips = range(0, cols, 2)

    def hops(sign):
        pairs = []
        for g in range(groups):
            for c in range(cols):
                step = -sign if c < cols // 2 else sign
                pairs.append((g * cols + c, (g + step) % groups * cols + c))
        return pairs

    near, far = hops(1), hops(-1)

    def to_group(value, pairs):
        return lax.ppermute(value, ("row", "col"), pairs)

    *sorted_blocks, current = sort_blocks(neighbours, blocks, start, cols)
    blks = []
    for m in chips:
        got = exchange(sorted_blocks[m // 2], m, "col") if m else sorted_blocks[0]
        blks += [got, exchange(got, 1, "col")]
    table = None
    for step in range(ITERS):
        own_chips = {m: exchange(current, m, "col") if m else current for m in chips}
        halo_chips = {m: to_group(own_chips[m], near if m < cols // 2 else far) for m in chips}
        owns, halos = [], []
        for m in chips:
            owns += [own_chips[m], exchange(own_chips[m], 1, "col")]
        for m in chips:
            halos += [halo_chips[m], exchange(halo_chips[m], 1, "col")]
        table, (keep_h, send_h, keep_o, send_o) = band(table, blks, owns, halos)

        def folded(keep, send):
            got = exchange(send, 1, "col")
            sums = [keep[i].astype(jnp.float32) + got[i].astype(jnp.float32) for i in range(cols // 2)]
            return [sums[0]] + [
                exchange(sums[m // 2].astype(jnp.bfloat16), m, "col") for m in chips if m
            ]

        halo_parts = folded(keep_h, send_h)
        halo_sum = halo_parts[0]
        for part in halo_parts[1:]:
            halo_sum = halo_sum + part.astype(jnp.float32)
        returned = to_group(halo_sum.astype(jnp.bfloat16), far)
        z, keep, send = gram(cols, *folded(keep_o, send_o), returned)
        g = summed(keep, send)
        last = step == ITERS - 1
        current, diagonal = orthonormal(
            g, z, jnp.float32 if last else jnp.bfloat16, math.sqrt(total_rows) if last else 1.0
        )
    return current, diagonal.reshape(width)


def solution(mesh):
    placed = (P("row", "col", None, None), P("row", "col"), P(("row", "col"), None))
    return jax.shard_map(
        per_device,
        mesh=mesh,
        in_specs=placed,
        out_specs=(P(("row", "col"), None), P()),
        check_vma=False,
    )
```

```python
import functools
import math

import jax
import jax.numpy as jnp
from jax import lax
from jax.experimental import pallas as pl
from jax.experimental.pallas import tpu as pltpu
from jax.sharding import PartitionSpec as P

ITERS = 2
PANEL = 64
GROUP = 8
HIGH = lax.Precision.HIGHEST
ANY = pl.BlockSpec(memory_space=pl.ANY)
SMEM = pl.BlockSpec(memory_space=pltpu.SMEM)
VMEM = pl.BlockSpec(memory_space=pltpu.VMEM)
BIG = 60 * 2**20
BAND = 28 * 2**20


def sort_kernel(cols, halves, slots, nb_ref, blk_ref, start_ref, *refs):
    outs, start_out = refs[: cols // 2], refs[cols // 2]
    held, rows, isem, osem = refs[cols // 2 + 1 :]
    half = held.shape[4]
    piece, width = start_ref.shape
    me = lax.axis_index("col")
    first = pltpu.make_async_copy(start_ref, rows.at[pl.ds(0, piece)], isem.at[cols * halves])
    first.start()
    ins = []
    for m in range(cols):
        to = jnp.bitwise_xor(me, m)
        for h in range(halves):
            at = to * halves + h
            ins.append(
                pltpu.make_async_copy(
                    blk_ref.at[at // 2, :, pl.ds(pl.multiple_of(at % 2 * half, half), half), :],
                    held.at[m // 2, m % 2, h],
                    isem.at[m * halves + h],
                )
            )
    for copy in ins:
        copy.start()
    lane = lax.broadcasted_iota(jnp.int32, (16, width), 1)
    numbers = jnp.zeros((16, width), jnp.float32)
    for i in range(halves * cols // 2):
        for n in range(slots):
            value = nb_ref[i, n].astype(jnp.float32)
            numbers = jnp.where(lane == i * slots + n, value, numbers)
    rows[piece:, :] = numbers.astype(rows.dtype)
    first.wait()
    copies = [pltpu.make_async_copy(rows, start_out, osem.at[cols // 2])]
    copies[0].start()
    for i in range(cols // 2):
        for copy in ins[2 * i * halves : 2 * (i + 1) * halves]:
            copy.wait()
        copies.append(pltpu.make_async_copy(held.at[i], outs[i], osem.at[i]))
        copies[-1].start()
    for copy in copies:
        copy.wait()


def sort_blocks(neighbours, blocks, start, cols):
    rows, slots, side, _ = blocks.shape
    halves = 2 * rows // cols
    piece, width = start.shape
    shape = (2, halves, slots, side // 2, side)
    return pl.pallas_call(
        functools.partial(sort_kernel, cols, halves, slots),
        out_shape=(jax.ShapeDtypeStruct(shape, blocks.dtype),) * (cols // 2)
        + (jax.ShapeDtypeStruct((piece + 16, width), start.dtype),),
        in_specs=[SMEM, ANY, ANY],
        out_specs=(ANY,) * (cols // 2 + 1),
        scratch_shapes=[
            pltpu.VMEM((cols // 2,) + shape, blocks.dtype),
            pltpu.VMEM((piece + 16, width), start.dtype),
            pltpu.SemaphoreType.DMA((cols * halves + 1,)),
            pltpu.SemaphoreType.DMA((cols // 2 + 1,)),
        ],
        compiler_params=pltpu.CompilerParams(vmem_limit_bytes=BIG),
        name="sort_blocks",
    )(neighbours, blocks, start)


def band_kernel(cols, first, *refs):
    known = not first
    held, refs = refs[:known], refs[known:]
    blks, owns, halos = refs[:cols], refs[cols : 2 * cols], refs[2 * cols : 3 * cols]
    keep_h, send_h, keep_o, send_o = refs[3 * cols : 3 * cols + 4]
    table, refs = (held if known else refs[3 * cols + 4 :])[0], refs[3 * cols + 4 + first :]
    xwin, zacc, yref, nbi, nb_ref, nsem = refs
    piece, width = keep_h.shape[1:]
    _, halves, slots, half, side = blks[0].shape
    low = cols // 2 * piece
    me = lax.axis_index("col")
    odd = me % 2

    def own_at(c):
        return pl.multiple_of(low + c * piece, half)

    def halo_at(c):
        return pl.multiple_of(
            jnp.where(c < cols // 2, low + (cols + c) * piece, (c - cols // 2) * piece), half
        )

    if first:
        for m in range(cols):
            nbi[m : m + 1, :] = owns[m][piece:, :].astype(jnp.float32)[:1].astype(jnp.int32)
        written = pltpu.make_async_copy(nbi, table, nsem.at[0])
        written.start()
        written.wait()
    numbers = pltpu.make_async_copy(table, nb_ref, nsem.at[0])
    numbers.start()
    for m in range(cols):
        c = jnp.bitwise_xor(me, m)
        xwin[pl.ds(own_at(c), piece), :] = owns[m][:piece, :]
        xwin[pl.ds(halo_at(c), piece), :] = halos[m][:piece, :]
    zacc[...] = jnp.zeros_like(zacc)
    numbers.wait()

    single = 2 - 2 * odd
    pair_row = (me * halves + odd) // 2
    single_row = (me * halves + single) // 2

    def places(m, n):
        a = nb_ref[m, pair_row * slots + n] * side
        b = nb_ref[m, single_row * slots + n] * side
        return pl.multiple_of(a, side), pl.multiple_of(b, side)

    acc = jnp.zeros((2 * half, width), jnp.float32)
    acc1 = jnp.zeros((half, width), jnp.float32)
    for m in range(cols):
        for n in range(slots):
            a, b = places(m, n)
            pair = blks[m][m % 2, pl.ds(odd, 2), n].reshape(2 * half, side)
            acc += jnp.dot(pair, xwin[pl.ds(a, side), :], preferred_element_type=jnp.float32)
            acc1 += jnp.dot(
                blks[m][m % 2, single, n], xwin[pl.ds(b, side), :], preferred_element_type=jnp.float32
            )
    yref[: 2 * half] = acc.astype(jnp.bfloat16)
    yref[2 * half :] = acc1.astype(jnp.bfloat16)
    y = yref[: 2 * half]
    y1 = yref[2 * half :]
    turned = (((0,), (0,)), ((), ()))

    for m in range(cols):
        for n in range(slots):
            a, b = places(m, n)
            pair = blks[m][m % 2, pl.ds(odd, 2), n].reshape(2 * half, side)
            zacc[pl.ds(a, side), :] += lax.dot_general(
                pair, y, turned, preferred_element_type=jnp.float32
            )
            zacc[pl.ds(b, side), :] += lax.dot_general(
                blks[m][m % 2, single, n], y1, turned, preferred_element_type=jnp.float32
            )
    for pair, at_of in (((keep_h, send_h), halo_at), ((keep_o, send_o), own_at)):
        for j in (1, 0):
            for i in range(cols // 2):
                at = at_of(jnp.bitwise_xor(me, 2 * i + j))
                pair[j][i] = zacc[pl.ds(at, piece), :].astype(jnp.bfloat16)


def band(table, blks, owns, halos):
    first = table is None
    cols = len(blks)
    _, halves, slots, half, side = blks[0].shape
    width = owns[0].shape[1]
    piece = halves * half
    window = 2 * cols * piece
    out = jax.ShapeDtypeStruct((cols // 2, piece, width), jnp.bfloat16)
    numbers = jax.ShapeDtypeStruct((cols, width), jnp.int32)
    results = pl.pallas_call(
        functools.partial(band_kernel, cols, first),
        out_shape=(out,) * 4 + (numbers,) * first,
        in_specs=[ANY] * (not first) + [VMEM] * (3 * cols),
        out_specs=(VMEM,) * 4 + (ANY,) * first,
        scratch_shapes=[
            pltpu.VMEM((window, width), jnp.bfloat16),
            pltpu.VMEM((window, width), jnp.float32),
            pltpu.VMEM((halves * half, width), jnp.bfloat16),
            pltpu.VMEM((cols, width), jnp.int32),
            pltpu.SMEM((cols, width), jnp.int32),
            pltpu.SemaphoreType.DMA((1,)),
        ],
        compiler_params=pltpu.CompilerParams(vmem_limit_bytes=BAND),
        cost_estimate=pl.CostEstimate(
            flops=4 * cols * halves * slots * half * side * width,
            bytes_accessed=12 * 2**20,
            transcendentals=0,
        ),
        name="band",
    )(*(() if first else (table,)), *blks, *owns, *halos)
    return (results[4] if first else table), results[:4]


def gram_kernel(*refs):
    parts, (z_ref, keep_ref, send_ref, g) = refs[:-4], refs[-4:]
    z = parts[0][...]
    for part in parts[1:]:
        z = z + part[...].astype(jnp.float32)
    z_ref[...] = z
    g[...] = lax.dot_general(
        z, z, (((0,), (0,)), ((), ())), precision=HIGH, preferred_element_type=jnp.float32
    )
    me = lax.axis_index("col")
    chips, rows, _ = keep_ref.shape
    for i in range(chips):
        for j, out in ((0, keep_ref), (1, send_ref)):
            at = pl.multiple_of(jnp.bitwise_xor(me, 2 * i + j) * rows, rows)
            out[i] = g[pl.ds(at, rows), :]


def gram(cols, *parts):
    shape = parts[0].shape
    width = shape[1]
    half = jax.ShapeDtypeStruct((cols // 2, width // cols, width), jnp.float32)
    return pl.pallas_call(
        gram_kernel,
        out_shape=(jax.ShapeDtypeStruct(shape, jnp.float32), half, half),
        scratch_shapes=[pltpu.VMEM((width, width), jnp.float32)],
        name="gram",
    )(*parts)


def panel(tiles, start, count):
    lanes = 128
    at, offset = start // lanes, start % lanes
    done = [[] for _ in tiles]
    for k in range(0, count, GROUP):
        left = count - k
        rows = lax.broadcasted_iota(jnp.int32, (left, lanes), 0)
        columns = [
            jnp.broadcast_to(tiles[at][:, offset + k + j : offset + k + j + 1], (left, lanes))
            for j in range(GROUP)
        ]
        heads = [[t[j : j + 1, :] for t in tiles] for j in range(GROUP)]
        pivots = jnp.ones((GROUP, lanes), jnp.float32)
        terms = []
        for j in range(GROUP):
            pivot = columns[j][j : j + 1, :]
            inverse = 1.0 / pivot
            scaled = [h * inverse for h in heads[j]]
            terms.append((jnp.where(rows > j, columns[j], 0.0), scaled))
            pivots = jnp.where(rows[:GROUP] == j, pivot, pivots)
            for i in range(j + 1, GROUP):
                factor = columns[j][i : i + 1, :]
                columns[i] = columns[i] - columns[j] * (factor * inverse)
                heads[i] = [h - factor * s for h, s in zip(heads[i], scaled)]
        scale = 1.0 / jnp.sqrt(pivots)
        for t in range(len(tiles)):
            total = tiles[t]
            for below, scaled in terms:
                total = total - below * scaled[t]
            done[t].append(total[:GROUP] * scale)
            tiles[t] = total[GROUP:]
    return [jnp.concatenate(part, axis=0) for part in done]


def orthonormal_kernel(factor, *refs):
    parts, (z_ref, q_ref, d_ref, m) = refs[:-4], refs[-4:]
    rows, width = parts[0].shape
    lanes = 128
    me = lax.axis_index("col")
    for i, part in enumerate(parts):
        at = pl.multiple_of(jnp.bitwise_xor(me, i) * rows, rows)
        m[pl.ds(at, rows), :width] = part[...]
    r = lax.broadcasted_iota(jnp.int32, (width, width), 0)
    c = lax.broadcasted_iota(jnp.int32, (width, width), 1)
    eye = (r == c).astype(jnp.float32)
    m[:, width:] = eye
    for start in range(0, width, PANEL):
        end = start + PANEL
        first = start // lanes
        used = list(range(first, width // lanes)) + list(
            range(width // lanes, width // lanes + (end + lanes - 1) // lanes)
        )
        tiles = [m[start:end, t * lanes : (t + 1) * lanes] for t in used]
        tiles = panel(tiles, start - first * lanes, PANEL)
        for t, value in zip(used, tiles):
            m[start:end, t * lanes : (t + 1) * lanes] = value
        if end < width:
            upper = jnp.concatenate(tiles, axis=1)
            left = upper[:, : width - first * lanes]
            update = lax.dot_general(
                left, upper, (((0,), (0,)), ((), ())), precision=HIGH,
                preferred_element_type=jnp.float32,
            )
            skip = end - first * lanes
            for i, t in enumerate(used):
                m[end:, t * lanes : (t + 1) * lanes] -= update[skip:, i * lanes : (i + 1) * lanes]
    d_ref[...] = jnp.sum(m[:, :width] * eye, axis=0, keepdims=True)
    q = lax.dot_general(
        z_ref[...], m[:, width:], (((1,), (1,)), ((), ())), precision=HIGH,
        preferred_element_type=jnp.float32,
    )
    q_ref[...] = (q * factor).astype(q_ref.dtype)


def orthonormal(parts, z, dtype, factor):
    width = z.shape[1]
    return pl.pallas_call(
        functools.partial(orthonormal_kernel, factor),
        out_shape=(
            jax.ShapeDtypeStruct(z.shape, dtype),
            jax.ShapeDtypeStruct((1, width), jnp.float32),
        ),
        scratch_shapes=[pltpu.VMEM((width, 2 * width), jnp.float32)],
        name="orthonormal",
    )(*parts, z)


def exchange(value, mask, axis):
    return lax.ppermute(value, axis, [(i, i ^ mask) for i in range(lax.axis_size(axis))])


def stages_of(count):
    if count == 32:
        return ((1, 2, 3), (4,), (8, 16, 24))
    return tuple((1 << i,) for i in range(count.bit_length() - 1))


def summed(keep, send):
    chips = keep.shape[0]
    got = exchange(send, 1, "col")
    sums = [keep[i] + got[i] for i in range(chips)]
    part = sums[0]
    for i in range(1, chips):
        part = part + exchange(sums[i], 2 * i, "col")
    for stage in stages_of(lax.axis_size("row")):
        others = [exchange(part, mask, "row") for mask in stage]
        part = part + others[0]
        if len(others) == 3:
            part = part + (others[1] + others[2])
    out = []
    for i in range(chips):
        rows = exchange(part, 2 * i, "col") if i else part
        out += [rows, exchange(rows, 1, "col")]
    return out


def per_device(blocks, neighbours, start):
    cols = lax.axis_size("col")
    groups = lax.axis_size("row")
    piece, width = start.shape
    total_rows = piece * cols * groups
    chips = range(0, cols, 2)

    def hops(sign):
        pairs = []
        for g in range(groups):
            for c in range(cols):
                step = -sign if c < cols // 2 else sign
                pairs.append((g * cols + c, (g + step) % groups * cols + c))
        return pairs

    near, far = hops(1), hops(-1)

    def to_group(value, pairs):
        return lax.ppermute(value, ("row", "col"), pairs)

    *sorted_blocks, current = sort_blocks(neighbours, blocks, start, cols)
    blks = []
    for m in chips:
        got = exchange(sorted_blocks[m // 2], m, "col") if m else sorted_blocks[0]
        blks += [got, exchange(got, 1, "col")]
    table = None
    for step in range(ITERS):
        own_chips = {m: exchange(current, m, "col") if m else current for m in chips}
        halo_chips = {m: to_group(own_chips[m], near if m < cols // 2 else far) for m in chips}
        owns, halos = [], []
        for m in chips:
            owns += [own_chips[m], exchange(own_chips[m], 1, "col")]
        for m in chips:
            halos += [halo_chips[m], exchange(halo_chips[m], 1, "col")]
        table, (keep_h, send_h, keep_o, send_o) = band(table, blks, owns, halos)

        def folded(keep, send):
            got = exchange(send, 1, "col")
            sums = [keep[i].astype(jnp.float32) + got[i].astype(jnp.float32) for i in range(cols // 2)]
            return [sums[0]] + [
                exchange(sums[m // 2].astype(jnp.bfloat16), m, "col") for m in chips if m
            ]

        halo_parts = folded(keep_h, send_h)
        halo_sum = halo_parts[0]
        for part in halo_parts[1:]:
            halo_sum = halo_sum + part.astype(jnp.float32)
        returned = to_group(halo_sum.astype(jnp.bfloat16), far)
        z, keep, send = gram(cols, *folded(keep_o, send_o), returned)
        g = summed(keep, send)
        last = step == ITERS - 1
        current, diagonal = orthonormal(
            g, z, jnp.float32 if last else jnp.bfloat16, math.sqrt(total_rows) if last else 1.0
        )
    return current, diagonal.reshape(width)


def solution(mesh):
    placed = (P("row", "col", None, None), P("row", "col"), P(("row", "col"), None))
    return jax.shard_map(
        per_device,
        mesh=mesh,
        in_specs=placed,
        out_specs=(P(("row", "col"), None), P()),
        check_vma=False,
    )
```

```python
import functools
import math

import jax
import jax.numpy as jnp
from jax import lax
from jax.experimental import pallas as pl
from jax.experimental.pallas import tpu as pltpu
from jax.sharding import PartitionSpec as P

ITERS = 2
PANEL = 64
GROUP = 8
HIGH = lax.Precision.HIGHEST
ANY = pl.BlockSpec(memory_space=pl.ANY)
SMEM = pl.BlockSpec(memory_space=pltpu.SMEM)
VMEM = pl.BlockSpec(memory_space=pltpu.VMEM)
SORT = 16 * 2**20
BAND = 28 * 2**20


def sort_kernel(cols, halves, slots, nb_ref, blk_ref, start_ref, *refs):
    outs, start_out = refs[: cols // 2], refs[cols // 2]
    half = outs[0].shape[3]
    piece, width = start_ref.shape
    me = lax.axis_index("col")
    start_out[:piece, :] = start_ref[...]
    for m in range(cols):
        to = jnp.bitwise_xor(me, m)
        for h in range(halves):
            at = to * halves + h
            from_row = pl.multiple_of(at % 2 * half, half)
            for n in range(slots):
                outs[m // 2][m % 2, h, n] = blk_ref[at // 2, n, pl.ds(from_row, half), :]
    lane = lax.broadcasted_iota(jnp.int32, (16, width), 1)
    numbers = jnp.zeros((16, width), jnp.float32)
    for i in range(halves * cols // 2):
        for n in range(slots):
            value = nb_ref[n, i].astype(jnp.float32)
            numbers = jnp.where(lane == i * slots + n, value, numbers)
    start_out[piece:, :] = numbers.astype(start_out.dtype)


def sort_blocks(neighbours, blocks, start, cols):
    rows, slots, side, _ = blocks.shape
    halves = 2 * rows // cols
    piece, width = start.shape
    shape = (2, halves, slots, side // 2, side)
    return pl.pallas_call(
        functools.partial(sort_kernel, cols, halves, slots),
        out_shape=(jax.ShapeDtypeStruct(shape, blocks.dtype),) * (cols // 2)
        + (jax.ShapeDtypeStruct((piece + 16, width), start.dtype),),
        in_specs=[SMEM, VMEM, VMEM],
        out_specs=(VMEM,) * (cols // 2 + 1),
        compiler_params=pltpu.CompilerParams(vmem_limit_bytes=SORT),
        name="sort_blocks",
    )(neighbours.T, blocks, start)


def band_kernel(cols, first, *refs):
    known = not first
    held, refs = refs[:known], refs[known:]
    blks, owns, halos = refs[:cols], refs[cols : 2 * cols], refs[2 * cols : 3 * cols]
    keep_h, send_h, keep_o, send_o = refs[3 * cols : 3 * cols + 4]
    table, refs = (held if known else refs[3 * cols + 4 :])[0], refs[3 * cols + 4 + first :]
    xwin, zacc, yref, nbi, nb_ref, nsem = refs
    piece, width = keep_h.shape[1:]
    _, halves, slots, half, side = blks[0].shape
    low = cols // 2 * piece
    me = lax.axis_index("col")
    odd = me % 2

    def own_at(c):
        return pl.multiple_of(low + c * piece, half)

    def halo_at(c):
        return pl.multiple_of(
            jnp.where(c < cols // 2, low + (cols + c) * piece, (c - cols // 2) * piece), half
        )

    if first:
        for m in range(cols):
            nbi[m : m + 1, :] = owns[m][piece:, :].astype(jnp.float32)[:1].astype(jnp.int32)
        written = pltpu.make_async_copy(nbi, table, nsem.at[0])
        written.start()
        written.wait()
    numbers = pltpu.make_async_copy(table, nb_ref, nsem.at[0])
    numbers.start()
    for m in range(cols):
        c = jnp.bitwise_xor(me, m)
        xwin[pl.ds(own_at(c), piece), :] = owns[m][:piece, :]
        xwin[pl.ds(halo_at(c), piece), :] = halos[m][:piece, :]
    zacc[...] = jnp.zeros_like(zacc)
    numbers.wait()

    single = 2 - 2 * odd
    pair_row = (me * halves + odd) // 2
    single_row = (me * halves + single) // 2

    def places(m, n):
        a = nb_ref[m, pair_row * slots + n] * side
        b = nb_ref[m, single_row * slots + n] * side
        return pl.multiple_of(a, side), pl.multiple_of(b, side)

    acc = jnp.zeros((2 * half, width), jnp.float32)
    acc1 = jnp.zeros((half, width), jnp.float32)
    for m in range(cols):
        for n in range(slots):
            a, b = places(m, n)
            pair = blks[m][m % 2, pl.ds(odd, 2), n].reshape(2 * half, side)
            acc += jnp.dot(pair, xwin[pl.ds(a, side), :], preferred_element_type=jnp.float32)
            acc1 += jnp.dot(
                blks[m][m % 2, single, n], xwin[pl.ds(b, side), :], preferred_element_type=jnp.float32
            )
    yref[: 2 * half] = acc.astype(jnp.bfloat16)
    yref[2 * half :] = acc1.astype(jnp.bfloat16)
    y = yref[: 2 * half]
    y1 = yref[2 * half :]
    turned = (((0,), (0,)), ((), ()))

    for m in range(cols):
        for n in range(slots):
            a, b = places(m, n)
            pair = blks[m][m % 2, pl.ds(odd, 2), n].reshape(2 * half, side)
            zacc[pl.ds(a, side), :] += lax.dot_general(
                pair, y, turned, preferred_element_type=jnp.float32
            )
            zacc[pl.ds(b, side), :] += lax.dot_general(
                blks[m][m % 2, single, n], y1, turned, preferred_element_type=jnp.float32
            )
    for pair, at_of in (((keep_h, send_h), halo_at), ((keep_o, send_o), own_at)):
        for j in (1, 0):
            for i in range(cols // 2):
                at = at_of(jnp.bitwise_xor(me, 2 * i + j))
                pair[j][i] = zacc[pl.ds(at, piece), :].astype(jnp.bfloat16)


def band(table, blks, owns, halos):
    first = table is None
    cols = len(blks)
    _, halves, slots, half, side = blks[0].shape
    width = owns[0].shape[1]
    piece = halves * half
    window = 2 * cols * piece
    out = jax.ShapeDtypeStruct((cols // 2, piece, width), jnp.bfloat16)
    numbers = jax.ShapeDtypeStruct((cols, width), jnp.int32)
    results = pl.pallas_call(
        functools.partial(band_kernel, cols, first),
        out_shape=(out,) * 4 + (numbers,) * first,
        in_specs=[ANY] * (not first) + [VMEM] * (3 * cols),
        out_specs=(VMEM,) * 4 + (ANY,) * first,
        scratch_shapes=[
            pltpu.VMEM((window, width), jnp.bfloat16),
            pltpu.VMEM((window, width), jnp.float32),
            pltpu.VMEM((halves * half, width), jnp.bfloat16),
            pltpu.VMEM((cols, width), jnp.int32),
            pltpu.SMEM((cols, width), jnp.int32),
            pltpu.SemaphoreType.DMA((1,)),
        ],
        compiler_params=pltpu.CompilerParams(vmem_limit_bytes=BAND),
        cost_estimate=pl.CostEstimate(
            flops=4 * cols * halves * slots * half * side * width,
            bytes_accessed=12 * 2**20,
            transcendentals=0,
        ),
        name="band",
    )(*(() if first else (table,)), *blks, *owns, *halos)
    return (results[4] if first else table), results[:4]


def gram_kernel(*refs):
    parts, (z_ref, keep_ref, send_ref, g) = refs[:-4], refs[-4:]
    z = parts[0][...]
    for part in parts[1:]:
        z = z + part[...].astype(jnp.float32)
    z_ref[...] = z
    g[...] = lax.dot_general(
        z, z, (((0,), (0,)), ((), ())), precision=HIGH, preferred_element_type=jnp.float32
    )
    me = lax.axis_index("col")
    chips, rows, _ = keep_ref.shape
    for i in range(chips):
        for j, out in ((0, keep_ref), (1, send_ref)):
            at = pl.multiple_of(jnp.bitwise_xor(me, 2 * i + j) * rows, rows)
            out[i] = g[pl.ds(at, rows), :]


def gram(cols, *parts):
    shape = parts[0].shape
    width = shape[1]
    half = jax.ShapeDtypeStruct((cols // 2, width // cols, width), jnp.float32)
    return pl.pallas_call(
        gram_kernel,
        out_shape=(jax.ShapeDtypeStruct(shape, jnp.float32), half, half),
        scratch_shapes=[pltpu.VMEM((width, width), jnp.float32)],
        name="gram",
    )(*parts)


def panel(tiles, start, count):
    lanes = 128
    at, offset = start // lanes, start % lanes
    done = [[] for _ in tiles]
    for k in range(0, count, GROUP):
        left = count - k
        rows = lax.broadcasted_iota(jnp.int32, (left, lanes), 0)
        columns = [
            jnp.broadcast_to(tiles[at][:, offset + k + j : offset + k + j + 1], (left, lanes))
            for j in range(GROUP)
        ]
        heads = [[t[j : j + 1, :] for t in tiles] for j in range(GROUP)]
        pivots = jnp.ones((GROUP, lanes), jnp.float32)
        terms = []
        for j in range(GROUP):
            pivot = columns[j][j : j + 1, :]
            inverse = 1.0 / pivot
            scaled = [h * inverse for h in heads[j]]
            terms.append((jnp.where(rows > j, columns[j], 0.0), scaled))
            pivots = jnp.where(rows[:GROUP] == j, pivot, pivots)
            for i in range(j + 1, GROUP):
                factor = columns[j][i : i + 1, :]
                columns[i] = columns[i] - columns[j] * (factor * inverse)
                heads[i] = [h - factor * s for h, s in zip(heads[i], scaled)]
        scale = 1.0 / jnp.sqrt(pivots)
        for t in range(len(tiles)):
            total = tiles[t]
            for below, scaled in terms:
                total = total - below * scaled[t]
            done[t].append(total[:GROUP] * scale)
            tiles[t] = total[GROUP:]
    return [jnp.concatenate(part, axis=0) for part in done]


def orthonormal_kernel(factor, *refs):
    parts, (z_ref, q_ref, d_ref, m) = refs[:-4], refs[-4:]
    rows, width = parts[0].shape
    lanes = 128
    me = lax.axis_index("col")
    for i, part in enumerate(parts):
        at = pl.multiple_of(jnp.bitwise_xor(me, i) * rows, rows)
        m[pl.ds(at, rows), :width] = part[...]
    r = lax.broadcasted_iota(jnp.int32, (width, width), 0)
    c = lax.broadcasted_iota(jnp.int32, (width, width), 1)
    eye = (r == c).astype(jnp.float32)
    m[:, width:] = eye
    for start in range(0, width, PANEL):
        end = start + PANEL
        first = start // lanes
        used = list(range(first, width // lanes)) + list(
            range(width // lanes, width // lanes + (end + lanes - 1) // lanes)
        )
        tiles = [m[start:end, t * lanes : (t + 1) * lanes] for t in used]
        tiles = panel(tiles, start - first * lanes, PANEL)
        for t, value in zip(used, tiles):
            m[start:end, t * lanes : (t + 1) * lanes] = value
        if end < width:
            upper = jnp.concatenate(tiles, axis=1)
            left = upper[:, : width - first * lanes]
            update = lax.dot_general(
                left, upper, (((0,), (0,)), ((), ())), precision=HIGH,
                preferred_element_type=jnp.float32,
            )
            skip = end - first * lanes
            for i, t in enumerate(used):
                m[end:, t * lanes : (t + 1) * lanes] -= update[skip:, i * lanes : (i + 1) * lanes]
    d_ref[...] = jnp.sum(m[:, :width] * eye, axis=0, keepdims=True)
    q = lax.dot_general(
        z_ref[...], m[:, width:], (((1,), (1,)), ((), ())), precision=HIGH,
        preferred_element_type=jnp.float32,
    )
    q_ref[...] = (q * factor).astype(q_ref.dtype)


def orthonormal(parts, z, dtype, factor):
    width = z.shape[1]
    return pl.pallas_call(
        functools.partial(orthonormal_kernel, factor),
        out_shape=(
            jax.ShapeDtypeStruct(z.shape, dtype),
            jax.ShapeDtypeStruct((1, width), jnp.float32),
        ),
        scratch_shapes=[pltpu.VMEM((width, 2 * width), jnp.float32)],
        name="orthonormal",
    )(*parts, z)


def exchange(value, mask, axis):
    return lax.ppermute(value, axis, [(i, i ^ mask) for i in range(lax.axis_size(axis))])


def stages_of(count):
    if count == 32:
        return ((1, 2, 3), (4,), (8, 16, 24))
    return tuple((1 << i,) for i in range(count.bit_length() - 1))


def summed(keep, send):
    chips = keep.shape[0]
    got = exchange(send, 1, "col")
    sums = [keep[i] + got[i] for i in range(chips)]
    part = sums[0]
    for i in range(1, chips):
        part = part + exchange(sums[i], 2 * i, "col")
    for stage in stages_of(lax.axis_size("row")):
        others = [exchange(part, mask, "row") for mask in stage]
        part = part + others[0]
        if len(others) == 3:
            part = part + (others[1] + others[2])
    out = []
    for i in range(chips):
        rows = exchange(part, 2 * i, "col") if i else part
        out += [rows, exchange(rows, 1, "col")]
    return out


def per_device(blocks, neighbours, start):
    cols = lax.axis_size("col")
    groups = lax.axis_size("row")
    piece, width = start.shape
    total_rows = piece * cols * groups
    chips = range(0, cols, 2)

    def hops(sign):
        pairs = []
        for g in range(groups):
            for c in range(cols):
                step = -sign if c < cols // 2 else sign
                pairs.append((g * cols + c, (g + step) % groups * cols + c))
        return pairs

    near, far = hops(1), hops(-1)

    def to_group(value, pairs):
        return lax.ppermute(value, ("row", "col"), pairs)

    *sorted_blocks, current = sort_blocks(neighbours, blocks, start, cols)
    blks = []
    for m in chips:
        got = exchange(sorted_blocks[m // 2], m, "col") if m else sorted_blocks[0]
        blks += [got, exchange(got, 1, "col")]
    table = None
    for step in range(ITERS):
        own_chips = {m: exchange(current, m, "col") if m else current for m in chips}
        halo_chips = {m: to_group(own_chips[m], near if m < cols // 2 else far) for m in chips}
        owns, halos = [], []
        for m in chips:
            owns += [own_chips[m], exchange(own_chips[m], 1, "col")]
        for m in chips:
            halos += [halo_chips[m], exchange(halo_chips[m], 1, "col")]
        table, (keep_h, send_h, keep_o, send_o) = band(table, blks, owns, halos)

        def folded(keep, send):
            got = exchange(send, 1, "col")
            sums = [keep[i].astype(jnp.float32) + got[i].astype(jnp.float32) for i in range(cols // 2)]
            return [sums[0]] + [
                exchange(sums[m // 2].astype(jnp.bfloat16), m, "col") for m in chips if m
            ]

        halo_parts = folded(keep_h, send_h)
        halo_sum = halo_parts[0]
        for part in halo_parts[1:]:
            halo_sum = halo_sum + part.astype(jnp.float32)
        returned = to_group(halo_sum.astype(jnp.bfloat16), far)
        z, keep, send = gram(cols, *folded(keep_o, send_o), returned)
        g = summed(keep, send)
        last = step == ITERS - 1
        current, diagonal = orthonormal(
            g, z, jnp.float32 if last else jnp.bfloat16, math.sqrt(total_rows) if last else 1.0
        )
    return current, diagonal.reshape(width)


def solution(mesh):
    placed = (P("row", "col", None, None), P("row", "col"), P(("row", "col"), None))
    return jax.shard_map(
        per_device,
        mesh=mesh,
        in_specs=placed,
        out_specs=(P(("row", "col"), None), P()),
        check_vma=False,
    )
```

```python
import functools
import math

import jax
import jax.numpy as jnp
from jax import lax
from jax.experimental import pallas as pl
from jax.experimental.pallas import tpu as pltpu
from jax.sharding import PartitionSpec as P

ITERS = 2
PANEL = 64
GROUP = 8
HIGH = lax.Precision.HIGHEST
ANY = pl.BlockSpec(memory_space=pl.ANY)
SMEM = pl.BlockSpec(memory_space=pltpu.SMEM)
VMEM = pl.BlockSpec(memory_space=pltpu.VMEM)
BAND = 12 * 2**20
SMALL = 8 * 2**20


def sort_kernel(cols, halves, slots, nb_ref, blk_ref, start_ref, *refs):
    outs, start_out = refs[: cols // 2], refs[cols // 2]
    half = outs[0].shape[3]
    piece, width = start_ref.shape
    me = lax.axis_index("col")
    start_out[:piece, :] = start_ref[...]
    for m in range(cols):
        to = jnp.bitwise_xor(me, m)
        for h in range(halves):
            at = to * halves + h
            from_row = pl.multiple_of(at % 2 * half, half)
            for n in range(slots):
                outs[m // 2][m % 2, h, n] = blk_ref[at // 2, n, pl.ds(from_row, half), :]
    lane = lax.broadcasted_iota(jnp.int32, (16, width), 1)
    numbers = jnp.zeros((16, width), jnp.float32)
    for i in range(halves * cols // 2):
        for n in range(slots):
            value = nb_ref[n, i].astype(jnp.float32)
            numbers = jnp.where(lane == i * slots + n, value, numbers)
    start_out[piece:, :] = numbers.astype(start_out.dtype)


def sort_blocks(neighbours, blocks, start, cols):
    rows, slots, side, _ = blocks.shape
    halves = 2 * rows // cols
    piece, width = start.shape
    shape = (2, halves, slots, side // 2, side)
    return pl.pallas_call(
        functools.partial(sort_kernel, cols, halves, slots),
        out_shape=(jax.ShapeDtypeStruct(shape, blocks.dtype),) * (cols // 2)
        + (jax.ShapeDtypeStruct((piece + 16, width), start.dtype),),
        in_specs=[SMEM, VMEM, VMEM],
        out_specs=(VMEM,) * (cols // 2 + 1),
        compiler_params=pltpu.CompilerParams(vmem_limit_bytes=SMALL),
        name="sort_blocks",
    )(neighbours.T, blocks, start)


def band_kernel(cols, first, *refs):
    known = not first
    held, refs = refs[:known], refs[known:]
    blks, owns, halos = refs[:cols], refs[cols : 2 * cols], refs[2 * cols : 3 * cols]
    keep_h, send_h, keep_o, send_o = refs[3 * cols : 3 * cols + 4]
    table, refs = (held if known else refs[3 * cols + 4 :])[0], refs[3 * cols + 4 + first :]
    xwin, zacc, yref, nbi, nb_ref, nsem = refs
    piece, width = keep_h.shape[1:]
    _, halves, slots, half, side = blks[0].shape
    low = cols // 2 * piece
    me = lax.axis_index("col")
    odd = me % 2

    def own_at(c):
        return pl.multiple_of(low + c * piece, half)

    def halo_at(c):
        return pl.multiple_of(
            jnp.where(c < cols // 2, low + (cols + c) * piece, (c - cols // 2) * piece), half
        )

    if first:
        for m in range(cols):
            nbi[m : m + 1, :] = owns[m][piece:, :].astype(jnp.float32)[:1].astype(jnp.int32)
        written = pltpu.make_async_copy(nbi, table, nsem.at[0])
        written.start()
        written.wait()
    numbers = pltpu.make_async_copy(table, nb_ref, nsem.at[0])
    numbers.start()
    for m in range(cols):
        c = jnp.bitwise_xor(me, m)
        xwin[pl.ds(own_at(c), piece), :] = owns[m][:piece, :]
        xwin[pl.ds(halo_at(c), piece), :] = halos[m][:piece, :]
    zacc[...] = jnp.zeros_like(zacc)
    numbers.wait()

    single = 2 - 2 * odd
    pair_row = (me * halves + odd) // 2
    single_row = (me * halves + single) // 2

    def places(m, n):
        a = nb_ref[m, pair_row * slots + n] * side
        b = nb_ref[m, single_row * slots + n] * side
        return pl.multiple_of(a, side), pl.multiple_of(b, side)

    acc = jnp.zeros((2 * half, width), jnp.float32)
    acc1 = jnp.zeros((half, width), jnp.float32)
    for m in range(cols):
        for n in range(slots):
            a, b = places(m, n)
            pair = blks[m][m % 2, pl.ds(odd, 2), n].reshape(2 * half, side)
            acc += jnp.dot(pair, xwin[pl.ds(a, side), :], preferred_element_type=jnp.float32)
            acc1 += jnp.dot(
                blks[m][m % 2, single, n], xwin[pl.ds(b, side), :], preferred_element_type=jnp.float32
            )
    yref[: 2 * half] = acc.astype(jnp.bfloat16)
    yref[2 * half :] = acc1.astype(jnp.bfloat16)
    y = yref[: 2 * half]
    y1 = yref[2 * half :]
    turned = (((0,), (0,)), ((), ()))

    for m in range(cols):
        for n in range(slots):
            a, b = places(m, n)
            pair = blks[m][m % 2, pl.ds(odd, 2), n].reshape(2 * half, side)
            zacc[pl.ds(a, side), :] += lax.dot_general(
                pair, y, turned, preferred_element_type=jnp.float32
            )
            zacc[pl.ds(b, side), :] += lax.dot_general(
                blks[m][m % 2, single, n], y1, turned, preferred_element_type=jnp.float32
            )
    for pair, at_of in (((keep_h, send_h), halo_at), ((keep_o, send_o), own_at)):
        for j in (1, 0):
            for i in range(cols // 2):
                at = at_of(jnp.bitwise_xor(me, 2 * i + j))
                pair[j][i] = zacc[pl.ds(at, piece), :].astype(jnp.bfloat16)


def band(table, blks, owns, halos):
    first = table is None
    cols = len(blks)
    _, halves, slots, half, side = blks[0].shape
    width = owns[0].shape[1]
    piece = halves * half
    window = 2 * cols * piece
    out = jax.ShapeDtypeStruct((cols // 2, piece, width), jnp.bfloat16)
    numbers = jax.ShapeDtypeStruct((cols, width), jnp.int32)
    results = pl.pallas_call(
        functools.partial(band_kernel, cols, first),
        out_shape=(out,) * 4 + (numbers,) * first,
        in_specs=[ANY] * (not first) + [VMEM] * (3 * cols),
        out_specs=(VMEM,) * 4 + (ANY,) * first,
        scratch_shapes=[
            pltpu.VMEM((window, width), jnp.bfloat16),
            pltpu.VMEM((window, width), jnp.float32),
            pltpu.VMEM((halves * half, width), jnp.bfloat16),
            pltpu.VMEM((cols, width), jnp.int32),
            pltpu.SMEM((cols, width), jnp.int32),
            pltpu.SemaphoreType.DMA((1,)),
        ],
        compiler_params=pltpu.CompilerParams(vmem_limit_bytes=BAND),
        cost_estimate=pl.CostEstimate(
            flops=4 * cols * halves * slots * half * side * width,
            bytes_accessed=12 * 2**20,
            transcendentals=0,
        ),
        name="band",
    )(*(() if first else (table,)), *blks, *owns, *halos)
    return (results[4] if first else table), results[:4]


def gram_kernel(*refs):
    parts, (z_ref, keep_ref, send_ref, g) = refs[:-4], refs[-4:]
    z = parts[0][...]
    for part in parts[1:]:
        z = z + part[...].astype(jnp.float32)
    z_ref[...] = z
    g[...] = lax.dot_general(
        z, z, (((0,), (0,)), ((), ())), precision=HIGH, preferred_element_type=jnp.float32
    )
    me = lax.axis_index("col")
    chips, rows, _ = keep_ref.shape
    for i in range(chips):
        for j, out in ((0, keep_ref), (1, send_ref)):
            at = pl.multiple_of(jnp.bitwise_xor(me, 2 * i + j) * rows, rows)
            out[i] = g[pl.ds(at, rows), :]


def gram(cols, *parts):
    shape = parts[0].shape
    width = shape[1]
    half = jax.ShapeDtypeStruct((cols // 2, width // cols, width), jnp.float32)
    return pl.pallas_call(
        gram_kernel,
        out_shape=(jax.ShapeDtypeStruct(shape, jnp.float32), half, half),
        scratch_shapes=[pltpu.VMEM((width, width), jnp.float32)],
        compiler_params=pltpu.CompilerParams(vmem_limit_bytes=SMALL),
        name="gram",
    )(*parts)


def panel(tiles, start, count):
    lanes = 128
    at, offset = start // lanes, start % lanes
    done = [[] for _ in tiles]
    for k in range(0, count, GROUP):
        left = count - k
        rows = lax.broadcasted_iota(jnp.int32, (left, lanes), 0)
        columns = [
            jnp.broadcast_to(tiles[at][:, offset + k + j : offset + k + j + 1], (left, lanes))
            for j in range(GROUP)
        ]
        heads = [[t[j : j + 1, :] for t in tiles] for j in range(GROUP)]
        pivots = jnp.ones((GROUP, lanes), jnp.float32)
        terms = []
        for j in range(GROUP):
            pivot = columns[j][j : j + 1, :]
            inverse = 1.0 / pivot
            scaled = [h * inverse for h in heads[j]]
            terms.append((jnp.where(rows > j, columns[j], 0.0), scaled))
            pivots = jnp.where(rows[:GROUP] == j, pivot, pivots)
            for i in range(j + 1, GROUP):
                factor = columns[j][i : i + 1, :]
                columns[i] = columns[i] - columns[j] * (factor * inverse)
                heads[i] = [h - factor * s for h, s in zip(heads[i], scaled)]
        scale = 1.0 / jnp.sqrt(pivots)
        for t in range(len(tiles)):
            total = tiles[t]
            for below, scaled in terms:
                total = total - below * scaled[t]
            done[t].append(total[:GROUP] * scale)
            tiles[t] = total[GROUP:]
    return [jnp.concatenate(part, axis=0) for part in done]


def orthonormal_kernel(factor, *refs):
    parts, (z_ref, q_ref, d_ref, m) = refs[:-4], refs[-4:]
    rows, width = parts[0].shape
    lanes = 128
    me = lax.axis_index("col")
    for i, part in enumerate(parts):
        at = pl.multiple_of(jnp.bitwise_xor(me, i) * rows, rows)
        m[pl.ds(at, rows), :width] = part[...]
    r = lax.broadcasted_iota(jnp.int32, (width, width), 0)
    c = lax.broadcasted_iota(jnp.int32, (width, width), 1)
    eye = (r == c).astype(jnp.float32)
    m[:, width:] = eye
    for start in range(0, width, PANEL):
        end = start + PANEL
        first = start // lanes
        used = list(range(first, width // lanes)) + list(
            range(width // lanes, width // lanes + (end + lanes - 1) // lanes)
        )
        tiles = [m[start:end, t * lanes : (t + 1) * lanes] for t in used]
        tiles = panel(tiles, start - first * lanes, PANEL)
        for t, value in zip(used, tiles):
            m[start:end, t * lanes : (t + 1) * lanes] = value
        if end < width:
            upper = jnp.concatenate(tiles, axis=1)
            left = upper[:, : width - first * lanes]
            update = lax.dot_general(
                left, upper, (((0,), (0,)), ((), ())), precision=HIGH,
                preferred_element_type=jnp.float32,
            )
            skip = end - first * lanes
            for i, t in enumerate(used):
                m[end:, t * lanes : (t + 1) * lanes] -= update[skip:, i * lanes : (i + 1) * lanes]
    d_ref[...] = jnp.sum(m[:, :width] * eye, axis=0, keepdims=True)
    q = lax.dot_general(
        z_ref[...], m[:, width:], (((1,), (1,)), ((), ())), precision=HIGH,
        preferred_element_type=jnp.float32,
    )
    q_ref[...] = (q * factor).astype(q_ref.dtype)


def orthonormal(parts, z, dtype, factor):
    width = z.shape[1]
    return pl.pallas_call(
        functools.partial(orthonormal_kernel, factor),
        out_shape=(
            jax.ShapeDtypeStruct(z.shape, dtype),
            jax.ShapeDtypeStruct((1, width), jnp.float32),
        ),
        scratch_shapes=[pltpu.VMEM((width, 2 * width), jnp.float32)],
        compiler_params=pltpu.CompilerParams(vmem_limit_bytes=SMALL),
        name="orthonormal",
    )(*parts, z)


def exchange(value, mask, axis):
    return lax.ppermute(value, axis, [(i, i ^ mask) for i in range(lax.axis_size(axis))])


def stages_of(count):
    if count == 32:
        return ((1, 2, 3), (4,), (8, 16, 24))
    return tuple((1 << i,) for i in range(count.bit_length() - 1))


def summed(keep, send):
    chips = keep.shape[0]
    got = exchange(send, 1, "col")
    sums = [keep[i] + got[i] for i in range(chips)]
    part = sums[0]
    for i in range(1, chips):
        part = part + exchange(sums[i], 2 * i, "col")
    for stage in stages_of(lax.axis_size("row")):
        others = [exchange(part, mask, "row") for mask in stage]
        part = part + others[0]
        if len(others) == 3:
            part = part + (others[1] + others[2])
    out = []
    for i in range(chips):
        rows = exchange(part, 2 * i, "col") if i else part
        out += [rows, exchange(rows, 1, "col")]
    return out


def per_device(blocks, neighbours, start):
    cols = lax.axis_size("col")
    groups = lax.axis_size("row")
    piece, width = start.shape
    total_rows = piece * cols * groups
    chips = range(0, cols, 2)

    def hops(sign):
        pairs = []
        for g in range(groups):
            for c in range(cols):
                step = -sign if c < cols // 2 else sign
                pairs.append((g * cols + c, (g + step) % groups * cols + c))
        return pairs

    near, far = hops(1), hops(-1)

    def to_group(value, pairs):
        return lax.ppermute(value, ("row", "col"), pairs)

    *sorted_blocks, current = sort_blocks(neighbours, blocks, start, cols)
    blks = []
    for m in chips:
        got = exchange(sorted_blocks[m // 2], m, "col") if m else sorted_blocks[0]
        blks += [got, exchange(got, 1, "col")]
    table = None
    for step in range(ITERS):
        own_chips = {m: exchange(current, m, "col") if m else current for m in chips}
        halo_chips = {m: to_group(own_chips[m], near if m < cols // 2 else far) for m in chips}
        owns, halos = [], []
        for m in chips:
            owns += [own_chips[m], exchange(own_chips[m], 1, "col")]
        for m in chips:
            halos += [halo_chips[m], exchange(halo_chips[m], 1, "col")]
        table, (keep_h, send_h, keep_o, send_o) = band(table, blks, owns, halos)

        def folded(keep, send):
            got = exchange(send, 1, "col")
            sums = [keep[i].astype(jnp.float32) + got[i].astype(jnp.float32) for i in range(cols // 2)]
            return [sums[0]] + [
                exchange(sums[m // 2].astype(jnp.bfloat16), m, "col") for m in chips if m
            ]

        halo_parts = folded(keep_h, send_h)
        halo_sum = halo_parts[0]
        for part in halo_parts[1:]:
            halo_sum = halo_sum + part.astype(jnp.float32)
        returned = to_group(halo_sum.astype(jnp.bfloat16), far)
        z, keep, send = gram(cols, *folded(keep_o, send_o), returned)
        g = summed(keep, send)
        last = step == ITERS - 1
        current, diagonal = orthonormal(
            g, z, jnp.float32 if last else jnp.bfloat16, math.sqrt(total_rows) if last else 1.0
        )
    return current, diagonal.reshape(width)


def solution(mesh):
    placed = (P("row", "col", None, None), P("row", "col"), P(("row", "col"), None))
    return jax.shard_map(
        per_device,
        mesh=mesh,
        in_specs=placed,
        out_specs=(P(("row", "col"), None), P()),
        check_vma=False,
    )
```

```python
import functools
import math

import jax
import jax.numpy as jnp
from jax import lax
from jax.experimental import pallas as pl
from jax.experimental.pallas import tpu as pltpu
from jax.sharding import PartitionSpec as P

ITERS = 2
PANEL = 64
GROUP = 8
HIGH = lax.Precision.HIGHEST
ANY = pl.BlockSpec(memory_space=pl.ANY)
SMEM = pl.BlockSpec(memory_space=pltpu.SMEM)
VMEM = pl.BlockSpec(memory_space=pltpu.VMEM)
BAND = 12 * 2**20
SMALL = 8 * 2**20


def sort_kernel(cols, halves, slots, nb_ref, blk_ref, start_ref, *refs):
    outs, start_out = refs[: cols // 2], refs[cols // 2]
    half = outs[0].shape[3]
    piece, width = start_ref.shape
    me = lax.axis_index("col")
    start_out[:piece, :] = start_ref[...]
    for m in range(cols):
        to = jnp.bitwise_xor(me, m)
        for h in range(halves):
            at = to * halves + h
            from_row = pl.multiple_of(at % 2 * half, half)
            for n in range(slots):
                outs[m // 2][m % 2, h, n] = blk_ref[at // 2, n, pl.ds(from_row, half), :]
    lane = lax.broadcasted_iota(jnp.int32, (16, width), 1)
    numbers = jnp.zeros((16, width), jnp.float32)
    for i in range(halves * cols // 2):
        for n in range(slots):
            value = nb_ref[n, i].astype(jnp.float32)
            numbers = jnp.where(lane == i * slots + n, value, numbers)
    start_out[piece:, :] = numbers.astype(start_out.dtype)


def sort_blocks(neighbours, blocks, start, cols):
    rows, slots, side, _ = blocks.shape
    halves = 2 * rows // cols
    piece, width = start.shape
    shape = (2, halves, slots, side // 2, side)
    return pl.pallas_call(
        functools.partial(sort_kernel, cols, halves, slots),
        out_shape=(jax.ShapeDtypeStruct(shape, blocks.dtype),) * (cols // 2)
        + (jax.ShapeDtypeStruct((piece + 16, width), start.dtype),),
        in_specs=[SMEM, VMEM, VMEM],
        out_specs=(VMEM,) * (cols // 2 + 1),
        compiler_params=pltpu.CompilerParams(vmem_limit_bytes=SMALL),
        name="sort_blocks",
    )(neighbours.T, blocks, start)


def band_kernel(cols, first, *refs):
    known = not first
    held, refs = refs[:known], refs[known:]
    blks, owns, halos = refs[:cols], refs[cols : 2 * cols], refs[2 * cols : 3 * cols]
    keep_h, send_h, keep_o, send_o = refs[3 * cols : 3 * cols + 4]
    table, refs = (held if known else refs[3 * cols + 4 :])[0], refs[3 * cols + 4 + first :]
    xwin, zacc, yref, nbi, nb_ref, nsem = refs
    piece, width = keep_h.shape[1:]
    _, halves, slots, half, side = blks[0].shape
    low = cols // 2 * piece
    me = lax.axis_index("col")
    odd = me % 2

    def own_at(c):
        return pl.multiple_of(low + c * piece, half)

    def halo_at(c):
        return pl.multiple_of(
            jnp.where(c < cols // 2, low + (cols + c) * piece, (c - cols // 2) * piece), half
        )

    if first:
        for m in range(cols):
            nbi[m : m + 1, :] = owns[m][piece:, :].astype(jnp.float32)[:1].astype(jnp.int32)
        written = pltpu.make_async_copy(nbi, table, nsem.at[0])
        written.start()
        written.wait()
    numbers = pltpu.make_async_copy(table, nb_ref, nsem.at[0])
    numbers.start()
    for m in range(cols):
        c = jnp.bitwise_xor(me, m)
        xwin[pl.ds(own_at(c), piece), :] = owns[m][:piece, :]
        xwin[pl.ds(halo_at(c), piece), :] = halos[m][:piece, :]
    zacc[...] = jnp.zeros_like(zacc)
    numbers.wait()

    single = 2 - 2 * odd
    pair_row = (me * halves + odd) // 2
    single_row = (me * halves + single) // 2

    def places(m, n):
        a = nb_ref[m, pair_row * slots + n] * side
        b = nb_ref[m, single_row * slots + n] * side
        return pl.multiple_of(a, side), pl.multiple_of(b, side)

    acc = jnp.zeros((2 * half, width), jnp.float32)
    acc1 = jnp.zeros((half, width), jnp.float32)
    for m in range(cols):
        for n in range(slots):
            a, b = places(m, n)
            pair = blks[m][m % 2, pl.ds(odd, 2), n].reshape(2 * half, side)
            acc += jnp.dot(pair, xwin[pl.ds(a, side), :], preferred_element_type=jnp.float32)
            acc1 += jnp.dot(
                blks[m][m % 2, single, n], xwin[pl.ds(b, side), :], preferred_element_type=jnp.float32
            )
    yref[: 2 * half] = acc.astype(jnp.bfloat16)
    yref[2 * half :] = acc1.astype(jnp.bfloat16)
    y = yref[: 2 * half]
    y1 = yref[2 * half :]
    turned = (((0,), (0,)), ((), ()))

    for m in range(cols):
        for n in range(slots):
            a, b = places(m, n)
            pair = blks[m][m % 2, pl.ds(odd, 2), n].reshape(2 * half, side)
            zacc[pl.ds(a, side), :] += lax.dot_general(
                pair, y, turned, preferred_element_type=jnp.float32
            )
            zacc[pl.ds(b, side), :] += lax.dot_general(
                blks[m][m % 2, single, n], y1, turned, preferred_element_type=jnp.float32
            )
    for pair, at_of in (((keep_h, send_h), halo_at), ((keep_o, send_o), own_at)):
        for j in (1, 0):
            for i in range(cols // 2):
                at = at_of(jnp.bitwise_xor(me, 2 * i + j))
                pair[j][i] = zacc[pl.ds(at, piece), :].astype(jnp.bfloat16)


def band(table, blks, owns, halos):
    first = table is None
    cols = len(blks)
    _, halves, slots, half, side = blks[0].shape
    width = owns[0].shape[1]
    piece = halves * half
    window = 2 * cols * piece
    out = jax.ShapeDtypeStruct((cols // 2, piece, width), jnp.bfloat16)
    numbers = jax.ShapeDtypeStruct((cols, width), jnp.int32)
    results = pl.pallas_call(
        functools.partial(band_kernel, cols, first),
        out_shape=(out,) * 4 + (numbers,) * first,
        in_specs=[ANY] * (not first) + [VMEM] * (3 * cols),
        out_specs=(VMEM,) * 4 + (ANY,) * first,
        scratch_shapes=[
            pltpu.VMEM((window, width), jnp.bfloat16),
            pltpu.VMEM((window, width), jnp.float32),
            pltpu.VMEM((halves * half, width), jnp.bfloat16),
            pltpu.VMEM((cols, width), jnp.int32),
            pltpu.SMEM((cols, width), jnp.int32),
            pltpu.SemaphoreType.DMA((1,)),
        ],
        compiler_params=pltpu.CompilerParams(vmem_limit_bytes=BAND),
        cost_estimate=pl.CostEstimate(
            flops=4 * cols * halves * slots * half * side * width,
            bytes_accessed=12 * 2**20,
            transcendentals=0,
        ),
        name="band",
    )(*(() if first else (table,)), *blks, *owns, *halos)
    return (results[4] if first else table), results[:4]


def gram_kernel(*refs):
    parts, (z_ref, keep_ref, send_ref, g) = refs[:-4], refs[-4:]
    z = parts[0][...]
    for part in parts[1:]:
        z = z + part[...].astype(jnp.float32)
    z_ref[...] = z
    g[...] = lax.dot_general(
        z, z, (((0,), (0,)), ((), ())), precision=HIGH, preferred_element_type=jnp.float32
    )
    me = lax.axis_index("col")
    chips, rows, _ = keep_ref.shape
    for i in range(chips):
        for j, out in ((0, keep_ref), (1, send_ref)):
            at = pl.multiple_of(jnp.bitwise_xor(me, 2 * i + j) * rows, rows)
            out[i] = g[pl.ds(at, rows), :]


def gram(cols, *parts):
    shape = parts[0].shape
    width = shape[1]
    half = jax.ShapeDtypeStruct((cols // 2, width // cols, width), jnp.float32)
    return pl.pallas_call(
        gram_kernel,
        out_shape=(jax.ShapeDtypeStruct(shape, jnp.float32), half, half),
        scratch_shapes=[pltpu.VMEM((width, width), jnp.float32)],
        compiler_params=pltpu.CompilerParams(vmem_limit_bytes=SMALL),
        name="gram",
    )(*parts)


def panel(tiles, start, count):
    lanes = 128
    at, offset = start // lanes, start % lanes
    done = [[] for _ in tiles]
    for k in range(0, count, GROUP):
        left = count - k
        rows = lax.broadcasted_iota(jnp.int32, (left, lanes), 0)
        columns = [
            jnp.broadcast_to(tiles[at][:, offset + k + j : offset + k + j + 1], (left, lanes))
            for j in range(GROUP)
        ]
        heads = [[t[j : j + 1, :] for t in tiles] for j in range(GROUP)]
        pivots = jnp.ones((GROUP, lanes), jnp.float32)
        terms = []
        for j in range(GROUP):
            pivot = columns[j][j : j + 1, :]
            inverse = 1.0 / pivot
            scaled = [h * inverse for h in heads[j]]
            terms.append((jnp.where(rows > j, columns[j], 0.0), scaled))
            pivots = jnp.where(rows[:GROUP] == j, pivot, pivots)
            for i in range(j + 1, GROUP):
                factor = columns[j][i : i + 1, :]
                columns[i] = columns[i] - columns[j] * (factor * inverse)
                heads[i] = [h - factor * s for h, s in zip(heads[i], scaled)]
        scale = 1.0 / jnp.sqrt(pivots)
        for t in range(len(tiles)):
            total = tiles[t]
            for below, scaled in terms:
                total = total - below * scaled[t]
            done[t].append(total[:GROUP] * scale)
            tiles[t] = total[GROUP:]
    return [jnp.concatenate(part, axis=0) for part in done]


def orthonormal_kernel(factor, *refs):
    parts, (z_ref, q_ref, d_ref, m) = refs[:-4], refs[-4:]
    rows, width = parts[0].shape
    lanes = 128
    me = lax.axis_index("col")
    for i, part in enumerate(parts):
        at = pl.multiple_of(jnp.bitwise_xor(me, i) * rows, rows)
        m[pl.ds(at, rows), :width] = part[...]
    r = lax.broadcasted_iota(jnp.int32, (width, width), 0)
    c = lax.broadcasted_iota(jnp.int32, (width, width), 1)
    eye = (r == c).astype(jnp.float32)
    m[:, width:] = eye
    for start in range(0, width, PANEL):
        end = start + PANEL
        first = start // lanes
        used = list(range(first, width // lanes)) + list(
            range(width // lanes, width // lanes + (end + lanes - 1) // lanes)
        )
        tiles = [m[start:end, t * lanes : (t + 1) * lanes] for t in used]
        tiles = panel(tiles, start - first * lanes, PANEL)
        for t, value in zip(used, tiles):
            m[start:end, t * lanes : (t + 1) * lanes] = value
        if end < width:
            upper = jnp.concatenate(tiles, axis=1)
            left = upper[:, : width - first * lanes]
            update = lax.dot_general(
                left, upper, (((0,), (0,)), ((), ())), precision=HIGH,
                preferred_element_type=jnp.float32,
            )
            skip = end - first * lanes
            for i, t in enumerate(used):
                m[end:, t * lanes : (t + 1) * lanes] -= update[skip:, i * lanes : (i + 1) * lanes]
    d_ref[...] = jnp.sum(m[:, :width] * eye, axis=0, keepdims=True)
    q = lax.dot_general(
        z_ref[...], m[:, width:], (((1,), (1,)), ((), ())), precision=HIGH,
        preferred_element_type=jnp.float32,
    )
    q_ref[...] = (q * factor).astype(q_ref.dtype)


def orthonormal(parts, z, dtype, factor):
    width = z.shape[1]
    return pl.pallas_call(
        functools.partial(orthonormal_kernel, factor),
        out_shape=(
            jax.ShapeDtypeStruct(z.shape, dtype),
            jax.ShapeDtypeStruct((1, width), jnp.float32),
        ),
        scratch_shapes=[pltpu.VMEM((width, 2 * width), jnp.float32)],
        compiler_params=pltpu.CompilerParams(vmem_limit_bytes=SMALL),
        name="orthonormal",
    )(*parts, z)


def exchange(value, mask, axis):
    return lax.ppermute(value, axis, [(i, i ^ mask) for i in range(lax.axis_size(axis))])


def stages_of(count):
    if count == 32:
        return ((1, 2, 3), (4,), (8, 16, 24))
    return tuple((1 << i,) for i in range(count.bit_length() - 1))


def summed(keep, send):
    chips = keep.shape[0]
    got = exchange(send, 1, "col")
    sums = [keep[i] + got[i] for i in range(chips)]
    part = sums[0]
    for i in range(1, chips):
        part = part + exchange(sums[i], 2 * i, "col")
    for stage in stages_of(lax.axis_size("row")):
        others = [exchange(part, mask, "row") for mask in stage]
        part = part + others[0]
        if len(others) == 3:
            part = part + (others[1] + others[2])
    out = []
    for i in range(chips):
        rows = exchange(part, 2 * i, "col") if i else part
        out += [rows, exchange(rows, 1, "col")]
    return out


def per_device(blocks, neighbours, start):
    cols = lax.axis_size("col")
    groups = lax.axis_size("row")
    piece, width = start.shape
    total_rows = piece * cols * groups
    chips = range(0, cols, 2)

    def hops(sign):
        pairs = []
        for g in range(groups):
            for c in range(cols):
                step = -sign if c < cols // 2 else sign
                pairs.append((g * cols + c, (g + step) % groups * cols + c))
        return pairs

    near, far = hops(1), hops(-1)

    def to_group(value, pairs):
        return lax.ppermute(value, ("row", "col"), pairs)

    *sorted_blocks, current = sort_blocks(neighbours, blocks, start, cols)
    blks = []
    for m in chips:
        got = exchange(sorted_blocks[m // 2], m, "col") if m else sorted_blocks[0]
        blks += [got, exchange(got, 1, "col")]
    table = None
    for step in range(ITERS):
        own_chips = {m: exchange(current, m, "col") if m else current for m in chips}
        if step == 0:
            halo_chips = {m: to_group(own_chips[m], near if m < cols // 2 else far) for m in chips}
        else:
            halo_chips = {m: to_group(current, [(a, b ^ m) for a, b in near]) for m in chips}
        owns, halos = [], []
        for m in chips:
            owns += [own_chips[m], exchange(own_chips[m], 1, "col")]
        for m in chips:
            halos += [halo_chips[m], exchange(halo_chips[m], 1, "col")]
        table, (keep_h, send_h, keep_o, send_o) = band(table, blks, owns, halos)

        def folded(keep, send):
            got = exchange(send, 1, "col")
            sums = [keep[i].astype(jnp.float32) + got[i].astype(jnp.float32) for i in range(cols // 2)]
            return [sums[0]] + [
                exchange(sums[m // 2].astype(jnp.bfloat16), m, "col") for m in chips if m
            ]

        halo_parts = folded(keep_h, send_h)
        halo_sum = halo_parts[0]
        for part in halo_parts[1:]:
            halo_sum = halo_sum + part.astype(jnp.float32)
        returned = to_group(halo_sum.astype(jnp.bfloat16), far)
        z, keep, send = gram(cols, *folded(keep_o, send_o), returned)
        g = summed(keep, send)
        last = step == ITERS - 1
        current, diagonal = orthonormal(
            g, z, jnp.float32 if last else jnp.bfloat16, math.sqrt(total_rows) if last else 1.0
        )
    return current, diagonal.reshape(width)


def solution(mesh):
    placed = (P("row", "col", None, None), P("row", "col"), P(("row", "col"), None))
    return jax.shard_map(
        per_device,
        mesh=mesh,
        in_specs=placed,
        out_specs=(P(("row", "col"), None), P()),
        check_vma=False,
    )
```
